512 devices in a mesh: fsdp: 64 (over z, y), tensor: 8 (over x, core).
Axes of the slice: x: 4, y: 8, z: 8, core: 2. Of those that a mesh axis runs over, the one named last changes fastest.
Arguments:
- momentum: bfloat16 [16384, 30720], P('fsdp', 'tensor'), may hold values from -12.5 to 12.5
- right_prev: bfloat16 [30720, 256], P(('tensor', 'fsdp')), may hold values from -4 to 4
Outputs:
- new_momentum: bfloat16 [16384, 30720], P('fsdp', 'tensor')
- left_factor: float32 [16384, 256], P('fsdp')
- right_factor: bfloat16 [30720, 256], P(('tensor', 'fsdp'))
The draws below stay inside these ranges and needn't reach their ends.
All inputs are finite; a program needn't handle non-finite values.
Results may differ from the reference program's by a relative error of at most 0.004.
Values may be sent and summed in bfloat16 or wider, within the bound.
A program may use at most 64 MiB of HBM per device.

```python
import math
import jax
import jax.numpy as jnp
from jax import lax

D = 16384
FF = 30720
RANK = 256


def draw_momentum(key, part):
    key = jax.random.fold_in(key, 11)
    keys = jax.random.split(key, 5)
    row_place = (jnp.arange(D, dtype=jnp.float32) / D)[:, None]
    col_place = (jnp.arange(FF, dtype=jnp.float32) / FF)[None, :]
    noise = jnp.clip(jax.random.normal(keys[0], (D, FF), jnp.float32), -3.0, 3.0)
    common = jnp.clip(jax.random.normal(keys[1], (D, 1), jnp.float32), -2.0, 2.0)
    along = jnp.clip(jax.random.normal(keys[2], (1, FF), jnp.float32), -2.0, 2.0)
    col_spread = jnp.exp(jax.random.uniform(keys[3], (1, FF), jnp.float32, math.log(0.2), 0.0))
    row_spread = jax.random.uniform(keys[4], (D, 1), jnp.float32, 0.6, 1.0)
    row_scale = (0.5 + row_place) * row_spread
    col_scale = (0.5 + col_place) * col_spread
    return (row_scale * col_scale * (0.5 * noise + 0.3 * common * along)).astype(jnp.bfloat16)


def block_levels(own_key, dims, pieces, smallest, top_value):
    factor_of, own = 1.0, jax.random.fold_in(own_key, 6)
    for dim, blocks in pieces:
        draws = jnp.exp(jax.random.uniform(jax.random.fold_in(own, dim), (blocks,), jnp.float32, smallest / len(pieces), top_value / len(pieces)))
        factor_of = factor_of * jnp.repeat(draws, dims[dim] // blocks).reshape([-1 if axis == dim else 1 for axis in range(len(dims))])
    return factor_of


def scatter_about(own_key, dims, spread, reach, pieces=(), kind=jnp.bfloat16):
    result = spread * jax.random.normal(own_key, dims, jnp.float32)
    if pieces:
        result = result * block_levels(own_key, dims, pieces, -0.22, 0.18)
    return jnp.clip(result, -reach, reach).astype(kind)


def setup_inputs(seed: int = 0) -> dict:
    splits = jax.random.split(jax.random.key(seed), 3)
    momentum = draw_momentum(jax.random.fold_in(splits[2], 71), 0)
    right_prev = scatter_about(splits[1], (FF, RANK), 1.0, 4.0, ((0, 512),))
    return {"momentum": momentum, "right_prev": right_prev}


def reference(momentum, right_prev):
    left_raw = jnp.dot(momentum.astype(jnp.float32), right_prev.astype(jnp.float32), preferred_element_type=jnp.float32)
    orthonormal, triangle = jnp.linalg.qr(left_raw)
    flips = jnp.where(jnp.diagonal(triangle) < 0, -1.0, 1.0).astype(orthonormal.dtype)
    left = orthonormal * flips[None, :]
    left_factor = math.sqrt(D) * left
    left_low = left.astype(jnp.bfloat16)
    right_raw = lax.dot_general(momentum.astype(jnp.float32), left_low.astype(jnp.float32), (((0,), (0,)), ((), ())), preferred_element_type=jnp.float32)
    column_scale = lax.rsqrt(lax.optimization_barrier(jnp.mean(right_raw * right_raw, axis=0)) + 1e-06)
    right_factor = (right_raw * column_scale[None, :]).astype(jnp.bfloat16)
    right_low = right_raw.astype(jnp.bfloat16)
    moment_blocks = momentum.reshape(16, D // 16, FF)
    left_blocks = left_low.reshape(16, D // 16, RANK)

    def correct_block(inputs_pair):
        moment_rows, left_rows = inputs_pair
        update = lax.dot_general(left_rows.astype(jnp.float32), right_low.astype(jnp.float32), (((1,), (1,)), ((), ())), preferred_element_type=jnp.float32)
        return (moment_rows.astype(jnp.float32) - 0.5 * update).astype(jnp.bfloat16)
    new_momentum = lax.map(correct_block, (moment_blocks, left_blocks)).reshape(D, FF)
    return (new_momentum, left_factor, right_factor)
```

```python
import math

import jax
import jax.numpy as jnp
from jax import lax
from jax.experimental import pallas as pl
from jax.experimental.pallas import tpu as pltpu
from jax.sharding import PartitionSpec as P

D = 16384
FF = 30720
RANK = 256
ROWS = 256
COLS = 3840
SHARE = 60
PAD = 64
N = 8
HALF = 128
MESH = pl.DeviceIdType.MESH
F32 = jnp.float32
BF16 = jnp.bfloat16
HIGHEST = lax.Precision.HIGHEST
VMEM_LIMIT = 56 * 1024 * 1024


def place():
    f, t = lax.axis_index("fsdp"), lax.axis_index("tensor")
    return lax.div(f, N), lax.rem(f, N), t


def up(i, d):
    return lax.rem(i + d, N)


def remote(src, dst, send, recv, z, y, t):
    return pltpu.make_async_remote_copy(
        src_ref=src,
        dst_ref=dst,
        send_sem=send,
        recv_sem=recv,
        device_id=(z * N + y, t),
        device_id_type=MESH,
    )


def greet(z, y, t):
    barrier = pltpu.get_barrier_semaphore()
    for d in range(1, N):
        for there in ((z, up(y, d), t), (up(z, d), y, t), (z, y, up(t, d))):
            pl.semaphore_signal(
                barrier, inc=1, device_id=(there[0] * N + there[1], there[2]), device_id_type=MESH
            )
    pl.semaphore_wait(barrier, 3 * (N - 1))


def exchange(axis, here, src_of, dst_of, send, recv):
    z, y, t = here
    me = here[axis]
    sent, waits = [], []
    for d in (4, 3, 5, 2, 6, 1, 7):
        peer = up(me, d)
        there = [z, y, t]
        there[axis] = peer
        copy = remote(src_of(peer), dst_of(me), send.at[d], recv.at[d], *there)
        copy.start()
        sent.append(copy)
        origin = up(me, N - d)
        waits.append(remote(src_of(peer), dst_of(origin), send.at[d], recv.at[d], *there))
    return sent, waits


def gather_first(here, buf, send, recv):
    z, y, _ = here
    one, one_waits = exchange(
        1, here, lambda p: buf.at[0, z, y], lambda i: buf.at[0, z, i], send.at[0], recv.at[0]
    )
    two, two_waits = exchange(
        0, here, lambda p: buf.at[1, z, y], lambda i: buf.at[1, i, y], send.at[1], recv.at[1]
    )
    return one + two, one_waits + two_waits


def strip(buf, half, i, unit):
    if half == 0:
        return buf.at[0, i, pl.ds(4 * unit, 4)]
    return buf.at[1, pl.ds(4 * unit, 4), i]


def ring_peer(here, half, way):
    z, y, t = here
    step = 1 if way == 0 else N - 1
    return (up(z, step), y, t) if half == 0 else (z, up(y, step), t)


STREAMS = [(unit, half, way) for unit in (0, 1) for half in (0, 1) for way in (0, 1)]


def gather_second(here, buf, send, recv):
    sent = []

    def arrived(half, way, s, unit):
        me = here[half]
        i = up(me, N - 1 - s) if way == 0 else up(me, 1 + s)
        dst = strip(buf, half, i, unit)
        remote(
            dst, dst, send.at[half, way, s, unit], recv.at[half, way, s, unit],
            *ring_peer(here, half, way),
        ).wait_recv()

    for s in range(4):
        for unit, half, way in STREAMS:
            if s == 3 and unit != way:
                continue
            if s > 0:
                arrived(half, way, s - 1, unit)
            me = here[half]
            i = up(me, N - s) if way == 0 else up(me, s)
            src = strip(buf, half, i, unit)
            copy = remote(
                src, src, send.at[half, way, s, unit], recv.at[half, way, s, unit],
                *ring_peer(here, half, way),
            )
            copy.start()
            sent.append(copy)
    for unit, half, way in STREAMS:
        if unit != way:
            arrived(half, way, 2, unit)
    for unit, half, way in STREAMS:
        if unit == way:
            arrived(half, way, 3, unit)
    return sent


def spread(offset, transposed):
    shape = (HALF, 256) if transposed else (256, HALF)
    n = lax.broadcasted_iota(jnp.int32, shape, 0 if transposed else 1)
    k = lax.broadcasted_iota(jnp.int32, shape, 1 if transposed else 0)
    high = n >= PAD
    want = offset + n - jnp.where(high, PAD - SHARE, 0)
    inside = n - jnp.where(high, PAD, 0) < SHARE
    return jnp.where((k == want) & inside, 1.0, 0.0).astype(BF16)


def first_kernel(
    m_ref, r_ref, left_ref, gram_ref, wide_ref,
    buf, mpad, part, got, gram, tile_y, tile_z,
    a_send, a_recv, b_send, b_recv, c_send, c_recv,
):
    here = place()
    z, y, t = here
    n = lax.broadcasted_iota(jnp.int32, (PAD, SHARE), 0)
    k = lax.broadcasted_iota(jnp.int32, (PAD, SHARE), 1)
    longer = jnp.where(n == k, 1.0, 0.0).astype(BF16)
    for half in (0, 1):
        buf[half, z, y] = jnp.dot(
            longer, r_ref[:, half * HALF:(half + 1) * HALF], preferred_element_type=F32
        ).astype(BF16)
    greet(z, y, t)
    sent, waits = gather_first(here, buf, a_send, a_recv)

    for i in range(COLS // 120):
        start = min(120 * i // 128 * 128, COLS - 256)
        window = m_ref[:, start:start + 256]
        mpad[:, i * 128:(i + 1) * 128] = jnp.dot(
            window, spread(120 * i - start, False), preferred_element_type=F32
        ).astype(BF16)
        wide_ref[i * 128:(i + 1) * 128, :] = lax.dot_general(
            spread(120 * i - start, True), window, (((1,), (1,)), ((), ())),
            preferred_element_type=F32,
        ).astype(BF16)

    for copy in waits:
        copy.wait_recv()
    sent += gather_second(here, buf, b_send, b_recv)

    width = N * PAD
    for half in (0, 1):
        total = jnp.zeros((ROWS, HALF), F32)
        for i in range(N):
            total += jnp.dot(
                mpad[:, i * width:(i + 1) * width],
                buf[half, i].reshape(width, HALF),
                preferred_element_type=F32,
            )
        part[:, half * HALF:(half + 1) * HALF] = total

    rows = ROWS // N
    piece = lambda i: pl.ds(pl.multiple_of(i * rows, rows), rows)
    more, waits = exchange(
        2, here, lambda p: part.at[piece(p)], lambda i: got.at[i], c_send.at[0], c_recv.at[0]
    )
    sent += more
    got[t] = part[piece(t), :]
    for copy in waits:
        copy.wait_recv()
    own = got[0]
    for i in range(1, N):
        own += got[i]
    left_ref[piece(t), :] = own
    more, waits = exchange(
        2, here, lambda p: left_ref.at[piece(t)], lambda i: left_ref.at[piece(i)],
        c_send.at[1], c_recv.at[1],
    )
    sent += more
    for copy in waits:
        copy.wait_recv()

    rows_all = left_ref[...]
    product = lax.dot_general(
        rows_all, rows_all, (((0,), (0,)), ((), ())),
        precision=HIGHEST, preferred_element_type=F32,
    )
    for i in range(64):
        r, c = i // 2 * 8, i % 2 * 128
        gram[i] = product[r:r + 8, c:c + 128]
    more, waits = exchange(
        1, here, lambda p: gram.at[t * N + p], lambda i: tile_y.at[i], c_send.at[2], c_recv.at[2]
    )
    sent += more
    tile_y[y] = gram[t * N + y]
    for copy in waits:
        copy.wait_recv()
    total = tile_y[0]
    for i in range(1, N):
        total += tile_y[i]
    tile_z[z] = total
    more, waits = exchange(
        0, here, lambda p: tile_z.at[z], lambda i: tile_z.at[i], c_send.at[3], c_recv.at[3]
    )
    sent += more
    for copy in waits:
        copy.wait_recv()
    total = tile_z[0]
    for i in range(1, N):
        total += tile_z[i]
    gram_ref[t * N + y] = total
    more, waits = exchange(
        1, here, lambda p: gram_ref.at[t * N + y], lambda i: gram_ref.at[t * N + i],
        c_send.at[4], c_recv.at[4],
    )
    sent += more
    for copy in waits:
        copy.wait_recv()
    block = lambda i: gram_ref.at[pl.ds(pl.multiple_of(i * N, N), N)]
    more, waits = exchange(
        2, here, lambda p: block(t), lambda i: block(i), c_send.at[5], c_recv.at[5]
    )
    sent += more
    for copy in waits:
        copy.wait_recv()
    for copy in sent:
        copy.wait_send()


def first(momentum, right_prev):
    dma = pltpu.SemaphoreType.DMA
    return pl.pallas_call(
        first_kernel,
        out_shape=(
            jax.ShapeDtypeStruct((ROWS, RANK), F32),
            jax.ShapeDtypeStruct((64, 8, 128), F32),
            jax.ShapeDtypeStruct((64 * PAD, ROWS), BF16),
        ),
        in_specs=[pl.BlockSpec(memory_space=pltpu.VMEM)] * 2,
        out_specs=[pl.BlockSpec(memory_space=pltpu.VMEM)] * 3,
        scratch_shapes=[
            pltpu.VMEM((2, N, N, PAD, HALF), BF16),
            pltpu.VMEM((ROWS, 64 * PAD), BF16),
            pltpu.VMEM((ROWS, RANK), F32),
            pltpu.VMEM((N, ROWS // N, RANK), F32),
            pltpu.VMEM((64, 8, 128), F32),
            pltpu.VMEM((N, 8, 128), F32),
            pltpu.VMEM((N, 8, 128), F32),
            dma((2, N)), dma((2, N)),
            dma((2, 2, 4, 2)), dma((2, 2, 4, 2)),
            dma((6, N)), dma((6, N)),
        ],
        compiler_params=pltpu.CompilerParams(
            collective_id=0, has_side_effects=True, vmem_limit_bytes=VMEM_LIMIT
        ),
    )(momentum, right_prev)


def invert_cholesky(w):
    lane = lax.broadcasted_iota(jnp.int32, (8, 128), 1)
    sub = lax.broadcasted_iota(jnp.int32, (8, 128), 0)
    row_of = lambda v, k: jnp.broadcast_to(v[k:k + 1, :], (8, 128))
    depth = 32
    for p in range(RANK // depth):
        base = p * depth
        b0 = base // 128
        rows = [
            [w[base + 8 * a:base + 8 * a + 8, 128 * b:128 * b + 128] for b in (0, 1)]
            for a in range(depth // 8)
        ]
        for q in range(depth // 8):
            l0 = (base + 8 * q) % 128
            below = range(q, depth // 8)
            cols = {
                a: [
                    jnp.broadcast_to(rows[a][b0][:, l0 + k:l0 + k + 1], (8, 128))
                    for k in range(8)
                ]
                for a in below
            }
            for k in range(8):
                inv = lax.rsqrt(row_of(cols[q][k], k))
                here = lane == l0 + k
                fresh = [row_of(rows[q][b], k) for b in (0, 1)]
                fresh[b0] = jnp.where(here, 1.0, fresh[b0])
                fresh = [v * inv for v in fresh]
                scaled = {k2: row_of(cols[q][k2], k) * inv for k2 in range(k + 1, 8)}
                for a in below:
                    mult = cols[a][k] * inv
                    if a == q:
                        mult = jnp.where(sub > k, mult, 0.0)
                    for b in (0, 1):
                        old = rows[a][b]
                        if b == b0:
                            erase = here & (sub > k) if a == q else here
                            old = jnp.where(erase, 0.0, old)
                        new = old - mult * fresh[b]
                        if a == q:
                            new = jnp.where(sub == k, fresh[b], new)
                        rows[a][b] = new
                    for k2 in range(k + 1, 8):
                        cols[a][k2] = cols[a][k2] - mult * scaled[k2]
        panel = jnp.concatenate([jnp.concatenate(r, axis=1) for r in rows], axis=0)
        w[base:base + depth, :] = panel
        end = base + depth
        if end < RANK:
            first_row = end // 128 * 128
            at = lax.broadcasted_iota(jnp.int32, (depth, RANK), 1) - base
            over = (at > lax.broadcasted_iota(jnp.int32, (depth, RANK), 0)) & (at < depth)
            update = lax.dot_general(
                panel[:, first_row:], jnp.where(over, 0.0, panel), (((0,), (0,)), ((), ())),
                precision=HIGHEST, preferred_element_type=F32,
            )[end - first_row:, :]
            col = lax.broadcasted_iota(jnp.int32, (RANK - end, RANK), 1)
            old = jnp.where((col >= base) & (col < end), 0.0, w[end:, :])
            w[end:, :] = old - update


def whiten_kernel(left_ref, gram_ref, factor_ref, low_ref, w):
    for i in range(64):
        r, c = i // 2 * 8, i % 2 * 128
        w[r:r + 8, c:c + 128] = gram_ref[i]
    invert_cholesky(w)
    row = lax.broadcasted_iota(jnp.int32, (RANK, RANK), 0)
    col = lax.broadcasted_iota(jnp.int32, (RANK, RANK), 1)
    inverse = jnp.where(col <= row, w[...], 0.0)
    left = lax.dot_general(
        left_ref[...], inverse, (((1,), (1,)), ((), ())),
        precision=HIGHEST, preferred_element_type=F32,
    )
    factor_ref[...] = math.sqrt(D) * left
    low_ref[...] = left.astype(BF16)


def whiten(left_raw, gram):
    return pl.pallas_call(
        whiten_kernel,
        out_shape=(
            jax.ShapeDtypeStruct((ROWS, RANK), F32),
            jax.ShapeDtypeStruct((ROWS, RANK), BF16),
        ),
        in_specs=[pl.BlockSpec(memory_space=pltpu.VMEM)] * 2,
        out_specs=[pl.BlockSpec(memory_space=pltpu.VMEM)] * 2,
        scratch_shapes=[pltpu.VMEM((RANK, RANK), F32)],
        compiler_params=pltpu.CompilerParams(vmem_limit_bytes=VMEM_LIMIT),
    )(left_raw, gram)


def last_kernel(
    m_ref, wide_ref, low_ref, new_ref, right_ref,
    part, away, land, near, rest, buf, packed, sq_y, sq_z, sq_t,
    a_send, a_recv, b_send, b_recv, r_send, r_recv, d_send, d_recv, s_send, s_recv,
):
    here = place()
    z, y, t = here
    low = low_ref[...]
    width = N * PAD
    for i in range(N):
        product = jnp.dot(
            wide_ref[i * width:(i + 1) * width, :], low, preferred_element_type=F32
        )
        for half in (0, 1):
            part[half, i] = product[:, half * HALF:(half + 1) * HALF].reshape(N, PAD, HALF)
    greet(z, y, t)
    sent = []

    def arrived(half, way, s, unit):
        dst = land.at[half, way, s, unit]
        remote(
            dst, dst, r_send.at[half, way, s, unit], r_recv.at[half, way, s, unit],
            *ring_peer(here, half, way),
        ).wait_recv()

    for s in range(4):
        for unit, half, way in STREAMS:
            if s == 0 and unit != way:
                continue
            me = here[half]
            dest = up(me, 4 - s) if way == 0 else up(me, 4 + s)
            own = strip(part, half, dest, unit)[...]
            if s == 0 or (s == 1 and unit != way):
                src = away.at[half, way, unit]
                src[...] = own.astype(BF16)
            else:
                arrived(half, way, s - 1, unit)
                src = land.at[half, way, s - 1, unit]
                src[...] = (src[...].astype(F32) + own).astype(BF16)
            copy = remote(
                src, land.at[half, way, s, unit],
                r_send.at[half, way, s, unit], r_recv.at[half, way, s, unit],
                *ring_peer(here, half, way),
            )
            copy.start()
            sent.append(copy)
    for half in (0, 1):
        for unit in (0, 1):
            for way in (0, 1):
                arrived(half, way, 3, unit)
            mine = strip(part, half, here[half], unit)
            near[half, pl.ds(4 * unit, 4)] = (
                mine[...]
                + land[half, 0, 3, unit].astype(F32)
                + land[half, 1, 3, unit].astype(F32)
            )
    share = []
    for half in (0, 1):
        more, waits = exchange(
            1 - half, here, lambda p: near.at[half, p], lambda i: rest.at[half, i],
            d_send.at[half], d_recv.at[half],
        )
        sent += more
        rest[half, here[1 - half]] = near[half, here[1 - half]]
        share.append(waits)
    for half in (0, 1):
        for copy in share[half]:
            copy.wait_recv()
        total = rest[half, 0]
        for i in range(1, N):
            total += rest[half, i]
        share[half] = total
        buf[half, z, y] = total.astype(BF16)

    more, gather_waits = gather_first(here, buf, a_send, a_recv)
    sent += more
    squares = [jnp.sum(v * v, axis=0, keepdims=True) for v in share]
    sq_y[y] = jnp.concatenate(squares + [jnp.zeros((6, HALF), F32)], axis=0)
    total = None
    for axis, tiles, after in ((1, sq_y, sq_z), (0, sq_z, sq_t)):
        me = here[axis]
        more, waits = exchange(
            axis, here, lambda p: tiles.at[me], lambda i: tiles.at[i],
            s_send.at[axis], s_recv.at[axis],
        )
        sent += more
        if axis == 0:
            for copy in gather_waits:
                copy.wait_recv()
        for copy in waits:
            copy.wait_recv()
        total = tiles[0]
        for i in range(1, N):
            total += tiles[i]
        after[here[0] if axis == 1 else t] = total
    more, square_waits = exchange(
        2, here, lambda p: sq_t.at[t], lambda i: sq_t.at[i], s_send.at[2], s_recv.at[2]
    )
    sent += more
    sent += gather_second(here, buf, b_send, b_recv)

    group = 4 * SHARE
    n = lax.broadcasted_iota(jnp.int32, (group, 256), 0)
    k = lax.broadcasted_iota(jnp.int32, (group, 256), 1)
    skip = sum(jnp.where(n >= SHARE * i, PAD - SHARE, 0) for i in (1, 2, 3))
    close = jnp.where(k == n + skip, 1.0, 0.0).astype(BF16)
    for g in range(16):
        for half in (0, 1):
            wide = buf[half, g // 2, g % 2 * 4:g % 2 * 4 + 4].reshape(256, HALF)
            packed[g * group:(g + 1) * group, half * HALF:(half + 1) * HALF] = jnp.dot(
                close, wide, preferred_element_type=F32
            ).astype(BF16)
    step = 768
    for i in range(COLS // step):
        update = lax.dot_general(
            low, packed[i * step:(i + 1) * step, :], (((1,), (1,)), ((), ())),
            preferred_element_type=F32,
        )
        block = m_ref[:, i * step:(i + 1) * step].astype(F32)
        new_ref[:, i * step:(i + 1) * step] = (block - 0.5 * update).astype(BF16)

    for copy in square_waits:
        copy.wait_recv()
    total = sq_t[0]
    for i in range(1, N):
        total += sq_t[i]
    scale = lax.rsqrt(total / FF + 1e-06)
    right = jnp.concatenate([share[0] * scale[0:1, :], share[1] * scale[1:2, :]], axis=1)
    right_ref[...] = right[:SHARE, :].astype(BF16)
    for copy in sent:
        copy.wait_send()


def last(momentum, wide, low):
    dma = pltpu.SemaphoreType.DMA
    return pl.pallas_call(
        last_kernel,
        out_shape=(
            jax.ShapeDtypeStruct((ROWS, COLS), BF16),
            jax.ShapeDtypeStruct((SHARE, RANK), BF16),
        ),
        in_specs=[pl.BlockSpec(memory_space=pltpu.VMEM)] * 3,
        out_specs=[pl.BlockSpec(memory_space=pltpu.VMEM)] * 2,
        scratch_shapes=[
            pltpu.VMEM((2, N, N, PAD, HALF), F32),
            pltpu.VMEM((2, 2, 2, 4, PAD, HALF), BF16),
            pltpu.VMEM((2, 2, 4, 2, 4, PAD, HALF), BF16),
            pltpu.VMEM((2, N, PAD, HALF), F32),
            pltpu.VMEM((2, N, PAD, HALF), F32),
            pltpu.VMEM((2, N, N, PAD, HALF), BF16),
            pltpu.VMEM((COLS, RANK), BF16),
            pltpu.VMEM((N, 8, 128), F32),
            pltpu.VMEM((N, 8, 128), F32),
            pltpu.VMEM((N, 8, 128), F32),
            dma((2, N)), dma((2, N)),
            dma((2, 2, 4, 2)), dma((2, 2, 4, 2)),
            dma((2, 2, 4, 2)), dma((2, 2, 4, 2)),
            dma((2, N)), dma((2, N)),
            dma((3, N)), dma((3, N)),
        ],
        compiler_params=pltpu.CompilerParams(
            collective_id=1, has_side_effects=True, vmem_limit_bytes=VMEM_LIMIT
        ),
    )(momentum, wide, low)


def body(momentum, right_prev):
    left_raw, gram, wide = first(momentum, right_prev)
    left_factor, low = whiten(left_raw, gram)
    new_momentum, right_factor = last(momentum, wide, low)
    return new_momentum, left_factor, right_factor


def solution(mesh):
    in_specs = (P("fsdp", "tensor"), P(("tensor", "fsdp"), None))
    out_specs = (P("fsdp", "tensor"), P("fsdp", None), P(("tensor", "fsdp"), None))
    return jax.shard_map(body, mesh=mesh, in_specs=in_specs, out_specs=out_specs, check_vma=False)
```

```python
import math

import jax
import jax.numpy as jnp
from jax import lax
from jax.experimental import pallas as pl
from jax.experimental.pallas import tpu as pltpu
from jax.sharding import PartitionSpec as P

D = 16384
FF = 30720
RANK = 256
ROWS = 256
COLS = 3840
SHARE = 60
PAD = 64
N = 8
HALF = 128
MESH = pl.DeviceIdType.MESH
F32 = jnp.float32
BF16 = jnp.bfloat16
HIGHEST = lax.Precision.HIGHEST
VMEM_LIMIT = 40 * 1024 * 1024


def place():
    f, t = lax.axis_index("fsdp"), lax.axis_index("tensor")
    return lax.div(f, N), lax.rem(f, N), t


def up(i, d):
    return lax.rem(i + d, N)


def remote(src, dst, send, recv, z, y, t):
    return pltpu.make_async_remote_copy(
        src_ref=src,
        dst_ref=dst,
        send_sem=send,
        recv_sem=recv,
        device_id=(z * N + y, t),
        device_id_type=MESH,
    )


def greet(z, y, t):
    barrier = pltpu.get_barrier_semaphore()
    for d in range(1, N):
        for there in ((z, up(y, d), t), (up(z, d), y, t), (z, y, up(t, d))):
            pl.semaphore_signal(
                barrier, inc=1, device_id=(there[0] * N + there[1], there[2]), device_id_type=MESH
            )
    pl.semaphore_wait(barrier, 3 * (N - 1))


def exchange(axis, here, src_of, dst_of, send, recv):
    z, y, t = here
    me = here[axis]
    sent, waits = [], []
    for d in (4, 3, 5, 2, 6, 1, 7):
        peer = up(me, d)
        there = [z, y, t]
        there[axis] = peer
        copy = remote(src_of(peer), dst_of(me), send.at[d], recv.at[d], *there)
        copy.start()
        sent.append(copy)
        origin = up(me, N - d)
        waits.append(remote(src_of(peer), dst_of(origin), send.at[d], recv.at[d], *there))
    return sent, waits


def strip(buf, half, i, unit):
    if half == 0:
        return buf.at[0, i, pl.ds(4 * unit, 4)]
    return buf.at[1, pl.ds(4 * unit, 4), i]


def ring_peer(here, half, way):
    z, y, t = here
    step = 1 if way == 0 else N - 1
    return (up(z, step), y, t) if half == 0 else (z, up(y, step), t)


SLOTS = (0, 1, 7, 2, 6, 3, 5, 4)
WAVES = ((0, 1), (1, 3), (4, 4))


def gather(here, rel, arrive, after, one_send, one_recv, two_send, two_recv):
    z, y, t = here
    sent, first = [], {}
    for slot in range(1, N):
        for half in (0, 1):
            there = list(here)
            there[1 - half] = up(here[1 - half], SLOTS[slot])
            copy = remote(
                rel.at[half, here[half], 0], rel.at[half, here[half], slot],
                one_send.at[half, slot], one_recv.at[half, slot], *there,
            )
            copy.start()
            sent.append(copy)
            first[half, slot] = copy

    def piece(half, way, s, wave):
        me = here[half]
        i = up(me, N - s) if way == 0 else up(me, s)
        start, count = WAVES[wave]
        return i, rel.at[half, i, pl.ds(start, count)]

    def ring(half, way, s, wave, src):
        return remote(
            src, src, two_send.at[half, way, s, wave], two_recv.at[half, way, s, wave],
            *ring_peer(here, half, way),
        )

    def arrived(half, way, s, wave):
        i, dst = piece(half, way, s + 1, wave)
        ring(half, way, s, wave, dst).wait_recv()
        return half, i, *WAVES[wave]

    forwards = lambda way, s, wave: s < 3 or (wave < 2) == (way == 0)
    for diag in range(6):
        came = []
        for wave in range(3):
            s = diag - wave
            if not 0 <= s < 4:
                continue
            for half in (0, 1):
                if s == 0:
                    start, count = WAVES[wave]
                    for slot in range(max(start, 1), start + count):
                        first[half, slot].wait_recv()
                    came.append((half, here[half], start, count))
                for way in (0, 1):
                    if not forwards(way, s, wave):
                        continue
                    if s > 0:
                        came.append(arrived(half, way, s - 1, wave))
                    copy = ring(half, way, s, wave, piece(half, way, s, wave)[1])
                    copy.start()
                    sent.append(copy)
        for chunk in came:
            arrive(*chunk)
        after(diag)
    for s in (2, 3):
        for wave in range(3):
            for half in (0, 1):
                for way in (0, 1):
                    if forwards(way, 3, wave) == (s == 3):
                        arrive(*arrived(half, way, s, wave))
    return sent


def placer(here, rel, buf):
    z, y, _ = here

    def arrive(half, i, start, count):
        for slot in range(start, start + count):
            origin = up(here[1 - half], N - SLOTS[slot])
            if half == 0:
                buf[0, i, origin] = rel[0, i, slot]
            else:
                buf[1, origin, i] = rel[1, i, slot]

    return arrive


def spread(offset, transposed):
    shape = (HALF, 256) if transposed else (256, HALF)
    n = lax.broadcasted_iota(jnp.int32, shape, 0 if transposed else 1)
    k = lax.broadcasted_iota(jnp.int32, shape, 1 if transposed else 0)
    high = n >= PAD
    want = offset + n - jnp.where(high, PAD - SHARE, 0)
    inside = n - jnp.where(high, PAD, 0) < SHARE
    return jnp.where((k == want) & inside, 1.0, 0.0).astype(BF16)


def invert_cholesky(w, between):
    lane = lax.broadcasted_iota(jnp.int32, (8, 128), 1)
    sub = lax.broadcasted_iota(jnp.int32, (8, 128), 0)
    row_of = lambda v, k: jnp.broadcast_to(v[k:k + 1, :], (8, 128))
    depth = 32
    for p in range(RANK // depth):
        base = p * depth
        b0 = base // 128
        rows = [
            [w[base + 8 * a:base + 8 * a + 8, 128 * b:128 * b + 128] for b in (0, 1)]
            for a in range(depth // 8)
        ]
        for q in range(depth // 8):
            l0 = (base + 8 * q) % 128
            below = range(q, depth // 8)
            cols = {
                a: [
                    jnp.broadcast_to(rows[a][b0][:, l0 + k:l0 + k + 1], (8, 128))
                    for k in range(8)
                ]
                for a in below
            }
            for k in range(8):
                inv = lax.rsqrt(row_of(cols[q][k], k))
                here = lane == l0 + k
                fresh = [row_of(rows[q][b], k) for b in (0, 1)]
                fresh[b0] = jnp.where(here, 1.0, fresh[b0])
                fresh = [v * inv for v in fresh]
                scaled = {k2: row_of(cols[q][k2], k) * inv for k2 in range(k + 1, 8)}
                for a in below:
                    mult = cols[a][k] * inv
                    if a == q:
                        mult = jnp.where(sub > k, mult, 0.0)
                    for b in (0, 1):
                        old = rows[a][b]
                        if b == b0:
                            erase = here & (sub > k) if a == q else here
                            old = jnp.where(erase, 0.0, old)
                        new = old - mult * fresh[b]
                        if a == q:
                            new = jnp.where(sub == k, fresh[b], new)
                        rows[a][b] = new
                    for k2 in range(k + 1, 8):
                        cols[a][k2] = cols[a][k2] - mult * scaled[k2]
        panel = jnp.concatenate([jnp.concatenate(r, axis=1) for r in rows], axis=0)
        w[base:base + depth, :] = panel
        end = base + depth
        if end < RANK:
            first_row = end // 128 * 128
            at = lax.broadcasted_iota(jnp.int32, (depth, RANK), 1) - base
            over = (at > lax.broadcasted_iota(jnp.int32, (depth, RANK), 0)) & (at < depth)
            update = lax.dot_general(
                panel[:, first_row:], jnp.where(over, 0.0, panel), (((0,), (0,)), ((), ())),
                precision=HIGHEST, preferred_element_type=F32,
            )[end - first_row:, :]
            col = lax.broadcasted_iota(jnp.int32, (RANK - end, RANK), 1)
            old = jnp.where((col >= base) & (col < end), 0.0, w[end:, :])
            w[end:, :] = old - update
        between(p)


def sums_kernel(
    m_ref, r_ref, left_ref, low_ref, packed_ref, right_ref,
    rel, rel2, buf, buf2, mpad, wide, part, raw, got, gram, summed, tile_y, tile_z, w, terms, land, near, rest,
    sq_y, sq_z, sq_t,
    a_send, a_recv, b_send, b_recv, c_send, c_recv, d_send, d_recv,
    e_send, e_recv, f_send, f_recv, r_send, r_recv, s_send, s_recv,
):
    here = place()
    z, y, t = here
    n = lax.broadcasted_iota(jnp.int32, (PAD, SHARE), 0)
    k = lax.broadcasted_iota(jnp.int32, (PAD, SHARE), 1)
    longer = jnp.where(n == k, 1.0, 0.0).astype(BF16)
    for half in (0, 1):
        rel[half, here[half], 0] = jnp.dot(
            longer, r_ref[:, half * HALF:(half + 1) * HALF], preferred_element_type=F32
        ).astype(BF16)
    greet(z, y, t)
    def widen(diag):
        if diag > 3:
            return
        for i in range(8 * diag, 8 * diag + 8):
            start = min(120 * i // 128 * 128, COLS - 256)
            window = m_ref[:, start:start + 256]
            mpad[:, i * 128:(i + 1) * 128] = jnp.dot(
                window, spread(120 * i - start, False), preferred_element_type=F32
            ).astype(BF16)
            wide[i * 128:(i + 1) * 128, :] = lax.dot_general(
                spread(120 * i - start, True), window, (((1,), (1,)), ((), ())),
                preferred_element_type=F32,
            ).astype(BF16)

    sent = gather(here, rel, placer(here, rel, buf), widen, a_send, a_recv, b_send, b_recv)

    width = N * PAD
    for half in (0, 1):
        total = jnp.zeros((ROWS, HALF), F32)
        for i in range(N):
            total += jnp.dot(
                mpad[:, i * width:(i + 1) * width],
                buf[half, i].reshape(width, HALF),
                preferred_element_type=F32,
            )
        part[:, half * HALF:(half + 1) * HALF] = total

    rows = ROWS // N
    piece = lambda i: pl.ds(pl.multiple_of(i * rows, rows), rows)
    more, waits = exchange(
        2, here, lambda p: part.at[piece(p)], lambda i: got.at[i], c_send.at[0], c_recv.at[0]
    )
    sent += more
    got[t] = part[piece(t), :]
    for copy in waits:
        copy.wait_recv()
    own = got[0]
    for i in range(1, N):
        own += got[i]
    raw[piece(t), :] = own
    more, waits = exchange(
        2, here, lambda p: raw.at[piece(t)], lambda i: raw.at[piece(i)],
        c_send.at[1], c_recv.at[1],
    )
    sent += more
    for copy in waits:
        copy.wait_recv()

    rows_all = raw[...]
    product = lax.dot_general(
        rows_all, rows_all, (((0,), (0,)), ((), ())),
        precision=HIGHEST, preferred_element_type=F32,
    )
    for i in range(64):
        r, c = i // 2 * 8, i % 2 * 128
        gram[i] = product[r:r + 8, c:c + 128]
    own_tile = t * N + y
    more, gram_waits = exchange(
        1, here, lambda p: gram.at[t * N + p], lambda i: tile_y.at[i], c_send.at[2], c_recv.at[2]
    )
    sent += more
    tile_y[y] = gram[own_tile]

    high = rows_all.astype(BF16)
    rows_all = rows_all - high.astype(F32)
    middle = rows_all.astype(BF16)
    lowest = (rows_all - middle.astype(F32)).astype(BF16)
    for i in range(N):
        block = wide[i * width:(i + 1) * width, :]
        total = jnp.dot(block, lowest, preferred_element_type=F32)
        total += jnp.dot(block, middle, preferred_element_type=F32)
        total += jnp.dot(block, high, preferred_element_type=F32)
        for half in (0, 1):
            terms[half, i] = total[:, half * HALF:(half + 1) * HALF].reshape(N, PAD, HALF)

    def order(way):
        a, b = way, 1 - way
        return ((0, a), (1, b), (1, a), (2, b), (2, a), (3, b), (3, a))

    def ring_send(half, way, s, unit, src):
        copy = remote(
            src, land.at[half, way, s, unit],
            r_send.at[half, way, s, unit], r_recv.at[half, way, s, unit],
            *ring_peer(here, half, way),
        )
        copy.start()
        sent.append(copy)

    def own_term(half, way, s, unit):
        me = here[half]
        return strip(terms, half, up(me, 4 - s) if way == 0 else up(me, 4 + s), unit)

    def tick(k):
        for half in (0, 1):
            for way in (0, 1):
                s, unit = order(way)[k]
                slot = land.at[half, way, s, unit]
                remote(
                    slot, slot, r_send.at[half, way, s, unit], r_recv.at[half, way, s, unit],
                    *ring_peer(here, half, way),
                ).wait_recv()
                if s < 3:
                    slot[...] = slot[...] + own_term(half, way, s + 1, unit)[...]
                    ring_send(half, way, s + 1, unit, slot)
                elif k == 5:
                    mine = strip(terms, half, here[half], unit)
                    near[half, pl.ds(4 * unit, 4)] = mine[...] + slot[...]
                else:
                    near[half, pl.ds(4 * unit, 4)] = near[half, pl.ds(4 * unit, 4)] + slot[...]

    for k in (0, 1):
        for half in (0, 1):
            for way in (0, 1):
                s, unit = order(way)[k]
                ring_send(half, way, s, unit, own_term(half, way, s, unit))

    def added(tiles):
        total = tiles[0]
        for i in range(1, N):
            total += tiles[i]
        return total

    def finish(waits):
        for copy in waits:
            copy.wait_recv()

    finish(gram_waits)
    tile_z[z] = added(tile_y)
    more, gram_waits = exchange(
        0, here, lambda p: tile_z.at[z], lambda i: tile_z.at[i], c_send.at[3], c_recv.at[3]
    )
    sent += more
    tick(0)
    tick(1)
    finish(gram_waits)
    summed[own_tile] = added(tile_z)
    more, gram_waits = exchange(
        1, here, lambda p: summed.at[own_tile], lambda i: summed.at[t * N + i],
        c_send.at[4], c_recv.at[4],
    )
    sent += more
    tick(2)
    finish(gram_waits)
    block = lambda i: summed.at[pl.ds(pl.multiple_of(i * N, N), N)]
    more, gram_waits = exchange(
        2, here, lambda p: block(t), lambda i: block(i), c_send.at[5], c_recv.at[5]
    )
    sent += more
    tick(3)
    finish(gram_waits)

    for i in range(64):
        r, c = i // 2 * 8, i % 2 * 128
        w[r:r + 8, c:c + 128] = summed[i]
    share_waits = []

    def between(p):
        if p < 3:
            tick(4 + p)
        if p == 2:
            for half in (0, 1):
                more, waits = exchange(
                    1 - half, here, lambda q: near.at[half, q], lambda i: rest.at[half, i],
                    d_send.at[half], d_recv.at[half],
                )
                sent.extend(more)
                share_waits.extend(waits)
                rest[half, here[1 - half]] = near[half, here[1 - half]]

    invert_cholesky(w, between)
    row = lax.broadcasted_iota(jnp.int32, (RANK, RANK), 0)
    col = lax.broadcasted_iota(jnp.int32, (RANK, RANK), 1)
    w[...] = jnp.where(col <= row, w[...], 0.0)
    solve = lambda rows: lax.dot_general(
        rows, w[...], (((1,), (1,)), ((), ())), precision=HIGHEST, preferred_element_type=F32
    )
    finish(share_waits)
    right = solve(jnp.concatenate([added(rest.at[0]), added(rest.at[1])], axis=1))
    for half in (0, 1):
        rel2[half, here[half], 0] = right[:, half * HALF:(half + 1) * HALF].astype(BF16)
    squares = jnp.sum(right * right, axis=0, keepdims=True)
    sq_y[y] = jnp.concatenate(
        [squares[:, :HALF], squares[:, HALF:], jnp.zeros((6, HALF), F32)], axis=0
    )
    square_waits = []

    def square_step(axis, tiles):
        me = here[axis]
        more, waits = exchange(
            axis, here, lambda p: tiles.at[me], lambda i: tiles.at[i],
            s_send.at[axis], s_recv.at[axis],
        )
        sent.extend(more)
        square_waits[:] = waits

    def beside(diag):
        if diag == 0:
            square_step(1, sq_y)
            left = solve(raw[...])
            left_ref[...] = left
            low_ref[...] = left.astype(BF16)
        elif diag == 2:
            finish(square_waits)
            sq_z[z] = added(sq_y)
            square_step(0, sq_z)
        elif diag == 4:
            finish(square_waits)
            sq_t[t] = added(sq_z)
            square_step(2, sq_t)

    sent += gather(here, rel2, placer(here, rel2, buf2), beside, e_send, e_recv, f_send, f_recv)

    group = 4 * SHARE
    n = lax.broadcasted_iota(jnp.int32, (group, 256), 0)
    k = lax.broadcasted_iota(jnp.int32, (group, 256), 1)
    skip = sum(jnp.where(n >= SHARE * i, PAD - SHARE, 0) for i in (1, 2, 3))
    close = jnp.where(k == n + skip, 1.0, 0.0).astype(BF16)
    for g in range(16):
        for half in (0, 1):
            wider = buf2[half, g // 2, g % 2 * 4:g % 2 * 4 + 4].reshape(256, HALF)
            packed_ref[g * group:(g + 1) * group, half * HALF:(half + 1) * HALF] = jnp.dot(
                close, wider, preferred_element_type=F32
            ).astype(BF16)

    finish(square_waits)
    total = added(sq_t)
    scale = lax.rsqrt(total / FF + 1e-06)
    right = jnp.concatenate(
        [right[:, :HALF] * scale[0:1, :], right[:, HALF:] * scale[1:2, :]], axis=1
    )
    right_ref[...] = right[:SHARE, :].astype(BF16)
    for copy in sent:
        copy.wait_send()


def sums(momentum, right_prev):
    dma = pltpu.SemaphoreType.DMA
    return pl.pallas_call(
        sums_kernel,
        out_shape=(
            jax.ShapeDtypeStruct((ROWS, RANK), F32),
            jax.ShapeDtypeStruct((ROWS, RANK), BF16),
            jax.ShapeDtypeStruct((COLS, RANK), BF16),
            jax.ShapeDtypeStruct((SHARE, RANK), BF16),
        ),
        in_specs=[pl.BlockSpec(memory_space=pltpu.VMEM)] * 2,
        out_specs=[pl.BlockSpec(memory_space=pltpu.VMEM)] * 4,
        scratch_shapes=[
            pltpu.VMEM((2, N, N, PAD, HALF), BF16),
            pltpu.VMEM((2, N, N, PAD, HALF), BF16),
            pltpu.VMEM((2, N, N, PAD, HALF), BF16),
            pltpu.VMEM((2, N, N, PAD, HALF), BF16),
            pltpu.VMEM((ROWS, 64 * PAD), BF16),
            pltpu.VMEM((64 * PAD, ROWS), BF16),
            pltpu.VMEM((ROWS, RANK), F32),
            pltpu.VMEM((ROWS, RANK), F32),
            pltpu.VMEM((N, ROWS // N, RANK), F32),
            pltpu.VMEM((64, 8, 128), F32),
            pltpu.VMEM((64, 8, 128), F32),
            pltpu.VMEM((N, 8, 128), F32),
            pltpu.VMEM((N, 8, 128), F32),
            pltpu.VMEM((RANK, RANK), F32),
            pltpu.VMEM((2, N, N, PAD, HALF), F32),
            pltpu.VMEM((2, 2, 4, 2, 4, PAD, HALF), F32),
            pltpu.VMEM((2, N, PAD, HALF), F32),
            pltpu.VMEM((2, N, PAD, HALF), F32),
            pltpu.VMEM((N, 8, 128), F32),
            pltpu.VMEM((N, 8, 128), F32),
            pltpu.VMEM((N, 8, 128), F32),
            dma((2, N)), dma((2, N)),
            dma((2, 2, 4, 3)), dma((2, 2, 4, 3)),
            dma((6, N)), dma((6, N)),
            dma((2, N)), dma((2, N)),
            dma((2, N)), dma((2, N)),
            dma((2, 2, 4, 3)), dma((2, 2, 4, 3)),
            dma((2, 2, 4, 2)), dma((2, 2, 4, 2)),
            dma((3, N)), dma((3, N)),
        ],
        compiler_params=pltpu.CompilerParams(
            collective_id=0, has_side_effects=True, vmem_limit_bytes=VMEM_LIMIT
        ),
    )(momentum, right_prev)


STEP = 768


def correct_kernel(
    m_ref, left_ref, low_ref, packed_ref, share_ref, new_ref, factor_ref, right_ref, tile, sem
):
    copies = []
    for i in range(COLS // STEP):
        part = pl.ds(i * STEP, STEP)
        update = lax.dot_general(
            low_ref[...], packed_ref[part, :], (((1,), (1,)), ((), ())),
            preferred_element_type=F32,
        )
        tile[i] = (m_ref[:, part].astype(F32) - 0.5 * update).astype(BF16)
        copy = pltpu.make_async_copy(tile.at[i], new_ref.at[:, part], sem.at[i])
        copy.start()
        copies.append(copy)
    factor_ref[...] = math.sqrt(D) * left_ref[...]
    right_ref[...] = share_ref[...]
    for copy in copies:
        copy.wait()


def correct(momentum, left, low, packed, share):
    vmem = pl.BlockSpec(memory_space=pltpu.VMEM)
    return pl.pallas_call(
        correct_kernel,
        out_shape=(
            jax.ShapeDtypeStruct((ROWS, COLS), BF16),
            jax.ShapeDtypeStruct((ROWS, RANK), F32),
            jax.ShapeDtypeStruct((SHARE, RANK), BF16),
        ),
        in_specs=[vmem] * 5,
        out_specs=(pl.BlockSpec(memory_space=pl.ANY), vmem, vmem),
        scratch_shapes=[
            pltpu.VMEM((COLS // STEP, ROWS, STEP), BF16),
            pltpu.SemaphoreType.DMA((COLS // STEP,)),
        ],
        compiler_params=pltpu.CompilerParams(vmem_limit_bytes=12 * 1024 * 1024),
    )(momentum, left, low, packed, share)


def body(momentum, right_prev):
    left, low, packed, share = sums(momentum, right_prev)
    return correct(momentum, left, low, packed, share)


def solution(mesh):
    in_specs = (P("fsdp", "tensor"), P(("tensor", "fsdp"), None))
    out_specs = (P("fsdp", "tensor"), P("fsdp", None), P(("tensor", "fsdp"), None))
    return jax.shard_map(body, mesh=mesh, in_specs=in_specs, out_specs=out_specs, check_vma=False)
```

```python
import math

import jax
import jax.numpy as jnp
from jax import lax
from jax.experimental import pallas as pl
from jax.experimental.pallas import tpu as pltpu
from jax.sharding import PartitionSpec as P

D = 16384
FF = 30720
RANK = 256
ROWS = 256
COLS = 3840
SHARE = 60
PAD = 64
N = 8
HALF = 128
MESH = pl.DeviceIdType.MESH
F32 = jnp.float32
BF16 = jnp.bfloat16
HIGHEST = lax.Precision.HIGHEST
VMEM_LIMIT = 40 * 1024 * 1024


def place():
    f, t = lax.axis_index("fsdp"), lax.axis_index("tensor")
    return lax.div(f, N), lax.rem(f, N), t


def up(i, d):
    return lax.rem(i + d, N)


def remote(src, dst, send, recv, z, y, t):
    return pltpu.make_async_remote_copy(
        src_ref=src,
        dst_ref=dst,
        send_sem=send,
        recv_sem=recv,
        device_id=(z * N + y, t),
        device_id_type=MESH,
    )


def greet(z, y, t):
    barrier = pltpu.get_barrier_semaphore()
    for d in range(1, N):
        for there in ((z, up(y, d), t), (up(z, d), y, t), (z, y, up(t, d))):
            pl.semaphore_signal(
                barrier, inc=1, device_id=(there[0] * N + there[1], there[2]), device_id_type=MESH
            )
    pl.semaphore_wait(barrier, 3 * (N - 1))


def exchange(axis, here, src_of, dst_of, view, send, recv):
    me = here[axis]
    for d in (4, 3, 5, 2, 6, 1, 7):
        there = list(here)
        there[axis] = up(me, d)
        remote(src_of(there[axis]), dst_of(me), send, recv, *there).start()
    return remote(view, view, send, recv, *there)


def strip(buf, half, i, unit):
    if half == 0:
        return buf.at[0, i, pl.ds(4 * unit, 4)]
    return buf.at[1, pl.ds(4 * unit, 4), i]


STREAMS = [(unit, half, way) for unit in (0, 1) for half in (0, 1) for way in (0, 1)]


def ring_peer(here, half, way):
    z, y, t = here
    step = 1 if way == 0 else N - 1
    return (up(z, step), y, t) if half == 0 else (z, up(y, step), t)


def gather_first(here, buf, one_send, one_recv):
    waits = []
    for half in (0, 1):
        base = here[half] * N
        own = buf.at[half, base + here[1 - half]]
        waits.append(exchange(
            1 - half, here, lambda p: own, lambda i: buf.at[half, base + i],
            buf.at[half, pl.ds(0, N - 1)], one_send.at[half], one_recv.at[half],
        ))
    return waits


def gather_second(here, buf, one_send, two_recv, after):
    def ring(half, way, s, unit, i):
        part = buf.at[half, pl.ds(pl.multiple_of(i * N + 4 * unit, 4), 4)]
        return remote(
            part, part, one_send.at[half], two_recv.at[half, way, s, unit],
            *ring_peer(here, half, way),
        )

    def arrived(half, way, s, unit):
        me = here[half]
        i = up(me, N - 1 - s) if way == 0 else up(me, 1 + s)
        ring(half, way, s, unit, i).wait_recv()

    for s in range(4):
        for unit, half, way in STREAMS:
            if s == 3 and unit != way:
                continue
            if s > 0:
                arrived(half, way, s - 1, unit)
            me = here[half]
            ring(half, way, s, unit, up(me, N - s) if way == 0 else up(me, s)).start()
        after(s)
    for s in (2, 3):
        for unit, half, way in STREAMS:
            if (unit == way) == (s == 3):
                arrived(half, way, s, unit)


def gather_sent(here, buf, one_send, one_recv):
    for half in (0, 1):
        view = buf.at[half, pl.ds(0, N * N - 1)]
        remote(view, view, one_send.at[half], one_recv.at[half], *ring_peer(here, half, 0)).wait_send()


def chunks(buf, half, z, ys):
    if half == 0:
        return buf[0, z * N + ys[0]:z * N + ys[-1] + 1].reshape(len(ys) * PAD, HALF)
    return jnp.concatenate([buf[1, y * N + z] for y in ys], axis=0)


def spread(offset, transposed):
    shape = (HALF, 256) if transposed else (256, HALF)
    n = lax.broadcasted_iota(jnp.int32, shape, 0 if transposed else 1)
    k = lax.broadcasted_iota(jnp.int32, shape, 1 if transposed else 0)
    high = n >= PAD
    want = offset + n - jnp.where(high, PAD - SHARE, 0)
    inside = n - jnp.where(high, PAD, 0) < SHARE
    return jnp.where((k == want) & inside, 1.0, 0.0).astype(BF16)


def invert_cholesky(w, between):
    lane = lax.broadcasted_iota(jnp.int32, (8, 128), 1)
    sub = lax.broadcasted_iota(jnp.int32, (8, 128), 0)
    row_of = lambda v, k: jnp.broadcast_to(v[k:k + 1, :], (8, 128))
    depth = 32
    for p in range(RANK // depth):
        base = p * depth
        b0 = base // 128
        rows = [
            [w[base + 8 * a:base + 8 * a + 8, 128 * b:128 * b + 128] for b in (0, 1)]
            for a in range(depth // 8)
        ]
        for q in range(depth // 8):
            l0 = (base + 8 * q) % 128
            below = range(q, depth // 8)
            cols = {
                a: [
                    jnp.broadcast_to(rows[a][b0][:, l0 + k:l0 + k + 1], (8, 128))
                    for k in range(8)
                ]
                for a in below
            }
            for k in range(8):
                inv = lax.rsqrt(row_of(cols[q][k], k))
                here = lane == l0 + k
                fresh = [row_of(rows[q][b], k) for b in (0, 1)]
                fresh[b0] = jnp.where(here, 1.0, fresh[b0])
                fresh = [v * inv for v in fresh]
                scaled = {k2: row_of(cols[q][k2], k) * inv for k2 in range(k + 1, 8)}
                for a in below:
                    mult = cols[a][k] * inv
                    if a == q:
                        mult = jnp.where(sub > k, mult, 0.0)
                    for b in (0, 1):
                        old = rows[a][b]
                        if b == b0:
                            erase = here & (sub > k) if a == q else here
                            old = jnp.where(erase, 0.0, old)
                        new = old - mult * fresh[b]
                        if a == q:
                            new = jnp.where(sub == k, fresh[b], new)
                        rows[a][b] = new
                    for k2 in range(k + 1, 8):
                        cols[a][k2] = cols[a][k2] - mult * scaled[k2]
        panel = jnp.concatenate([jnp.concatenate(r, axis=1) for r in rows], axis=0)
        w[base:base + depth, :] = panel
        end = base + depth
        if end < RANK:
            first_row = end // 128 * 128
            at = lax.broadcasted_iota(jnp.int32, (depth, RANK), 1) - base
            over = (at > lax.broadcasted_iota(jnp.int32, (depth, RANK), 0)) & (at < depth)
            update = lax.dot_general(
                panel[:, first_row:], jnp.where(over, 0.0, panel), (((0,), (0,)), ((), ())),
                precision=HIGHEST, preferred_element_type=F32,
            )[end - first_row:, :]
            col = lax.broadcasted_iota(jnp.int32, (RANK - end, RANK), 1)
            old = jnp.where((col >= base) & (col < end), 0.0, w[end:, :])
            w[end:, :] = old - update
        between(p)


def sums_kernel(
    m_hbm, r_hbm, left_ref, low_ref, packed_ref, right_ref,
    m_ref, r_ref, buf, buf2, mpad, wide, part, raw, got, gram, summed, tile_y, tile_z, w, terms, land,
    near, rest, sq_t,
    load, a_send, a_recv, b_recv, c_send, c_recv, d_send, d_recv,
    e_send, e_recv, f_recv, r_send, r_recv,
):
    here = place()
    z, y, t = here
    load_r = pltpu.make_async_copy(r_hbm, r_ref, load.at[0])
    load_m = pltpu.make_async_copy(m_hbm, m_ref, load.at[1])
    load_r.start()
    load_m.start()
    greet(z, y, t)
    load_r.wait()
    n = lax.broadcasted_iota(jnp.int32, (PAD, SHARE), 0)
    k = lax.broadcasted_iota(jnp.int32, (PAD, SHARE), 1)
    longer = jnp.where(n == k, 1.0, 0.0).astype(BF16)
    own = jnp.dot(longer, r_ref[...], preferred_element_type=F32).astype(BF16)
    for half in (0, 1):
        buf[half, here[half] * N + here[1 - half]] = own[:, half * HALF:(half + 1) * HALF]
    waits = gather_first(here, buf, a_send, a_recv)

    load_m.wait()

    def widen(tiles, transposed):
        for i in tiles:
            start = min(120 * i // 128 * 128, COLS - 256)
            window = m_ref[:, start:start + 256]
            if transposed:
                wide[i * 128:(i + 1) * 128, :] = lax.dot_general(
                    spread(120 * i - start, True), window, (((1,), (1,)), ((), ())),
                    preferred_element_type=F32,
                ).astype(BF16)
            else:
                mpad[:, i * 128:(i + 1) * 128] = jnp.dot(
                    window, spread(120 * i - start, False), preferred_element_type=F32
                ).astype(BF16)

    widen(range(16), False)
    for wait in waits:
        wait.wait_recv()

    def beside(s):
        if s == 0:
            widen(range(16, 32), False)
        else:
            widen(range(11 * s - 11, min(11 * s, 32)), True)

    gather_second(here, buf, a_send, b_recv, beside)

    width = N * PAD
    total = jnp.zeros((ROWS, RANK), F32)
    for i in range(N):
        block = jnp.concatenate([chunks(buf, half, i, range(N)) for half in (0, 1)], axis=1)
        total += jnp.dot(
            mpad[:, i * width:(i + 1) * width], block, preferred_element_type=F32
        )
    part[...] = total

    def begin(axis, src_of, dst_of, view, k):
        return exchange(axis, here, src_of, dst_of, view, c_send.at[k], c_recv.at[k])

    def added(tiles):
        total = tiles[0]
        for i in range(1, N):
            total += tiles[i]
        return total

    rows = ROWS // N
    piece = lambda i: pl.ds(pl.multiple_of(i * rows, rows), rows)
    seven = pl.ds(0, N - 1)
    sent = [begin(2, lambda p: part.at[piece(p)], lambda i: got.at[i], got.at[seven], 0)]
    got[t] = part[piece(t), :]
    sent[-1].wait_recv()
    raw[piece(t), :] = added(got)
    sent.append(begin(
        2, lambda p: raw.at[piece(t)], lambda i: raw.at[piece(i)], raw.at[pl.ds(0, 7 * rows)], 1
    ))
    sent[-1].wait_recv()

    rows_all = raw[...]
    product = lax.dot_general(
        rows_all, rows_all, (((0,), (0,)), ((), ())),
        precision=HIGHEST, preferred_element_type=F32,
    )
    for i in range(64):
        r, c = i // 2 * 8, i % 2 * 128
        gram[i] = product[r:r + 8, c:c + 128]
    own_tile = t * N + y
    sent.append(begin(
        1, lambda p: gram.at[t * N + p], lambda i: tile_y.at[i], tile_y.at[seven], 2
    ))
    tile_y[y] = gram[own_tile]

    high = rows_all.astype(BF16)
    rows_all = rows_all - high.astype(F32)
    middle = rows_all.astype(BF16)
    lowest = (rows_all - middle.astype(F32)).astype(BF16)
    for i in range(N):
        block = wide[i * width:(i + 1) * width, :]
        total = jnp.dot(block, lowest, preferred_element_type=F32)
        total += jnp.dot(block, middle, preferred_element_type=F32)
        total += jnp.dot(block, high, preferred_element_type=F32)
        for half in (0, 1):
            terms[half, i] = total[:, half * HALF:(half + 1) * HALF].reshape(N, PAD, HALF)

    def order(way):
        a, b = way, 1 - way
        return ((0, a), (1, b), (1, a), (2, b), (2, a), (3, b), (3, a))

    def ring_copy(half, way, k, src):
        return remote(
            src, land.at[half, way * 7 + k], r_send, r_recv.at[half, way * 7 + k],
            *ring_peer(here, half, way),
        )

    def own_term(half, way, s, unit):
        me = here[half]
        return strip(terms, half, up(me, 4 - s) if way == 0 else up(me, 4 + s), unit)

    def tick(k):
        for half in (0, 1):
            for way in (0, 1):
                s, unit = order(way)[k]
                slot = land.at[half, way * 7 + k]
                ring_copy(half, way, k, slot).wait_recv()
                if s < 3:
                    slot[...] = slot[...] + own_term(half, way, s + 1, unit)[...]
                    ring_copy(half, way, k + 2, slot).start()
                elif k == 5:
                    mine = strip(terms, half, here[half], unit)
                    near[half, pl.ds(4 * unit, 4)] = mine[...] + slot[...]
                else:
                    near[half, pl.ds(4 * unit, 4)] = near[half, pl.ds(4 * unit, 4)] + slot[...]

    def ring_start(k):
        for half in (0, 1):
            for way in (0, 1):
                s, unit = order(way)[k]
                ring_copy(half, way, k, own_term(half, way, s, unit)).start()

    sent[-1].wait_recv()
    tile_z[z] = added(tile_y)
    sent.append(begin(
        0, lambda p: tile_z.at[z], lambda i: tile_z.at[i], tile_z.at[seven], 3
    ))
    ring_start(0)
    sent[-1].wait_recv()
    summed[own_tile] = added(tile_z)
    sent.append(begin(
        1, lambda p: summed.at[own_tile], lambda i: summed.at[t * N + i], summed.at[seven], 4
    ))
    ring_start(1)
    tick(0)
    sent[-1].wait_recv()
    block = lambda i: summed.at[pl.ds(pl.multiple_of(i * N, N), N)]
    sent.append(begin(
        2, lambda p: block(t), lambda i: block(i), summed.at[pl.ds(0, 7 * N)], 5
    ))
    tick(1)
    sent[-1].wait_recv()

    for i in range(64):
        r, c = i // 2 * 8, i % 2 * 128
        w[r:r + 8, c:c + 128] = summed[i]
    share_waits = []

    def between(p):
        if p < 5:
            tick(2 + p)
        if p == 4:
            for half in (0, 1):
                share_waits.append(exchange(
                    1 - half, here, lambda q: near.at[half, q], lambda i: rest.at[half, i],
                    rest.at[half, seven], d_send.at[half], d_recv.at[half],
                ))
                rest[half, here[1 - half]] = near[half, here[1 - half]]

    invert_cholesky(w, between)
    row = lax.broadcasted_iota(jnp.int32, (RANK, RANK), 0)
    col = lax.broadcasted_iota(jnp.int32, (RANK, RANK), 1)
    w[...] = jnp.where(col <= row, w[...], 0.0)
    solve = lambda rows: lax.dot_general(
        rows, w[...], (((1,), (1,)), ((), ())), precision=HIGHEST, preferred_element_type=F32
    )
    for wait in share_waits:
        wait.wait_recv()
    right = solve(jnp.concatenate([added(rest.at[0]), added(rest.at[1])], axis=1))

    squares = jnp.sum(right * right, axis=0, keepdims=True)
    row = lax.broadcasted_iota(jnp.int32, (PAD, RANK), 0)
    chunk = jnp.where(row < SHARE, right, 0.0)
    for i in range(3):
        piece_of = squares.astype(BF16).astype(F32)
        squares = squares - piece_of
        chunk = jnp.where(row == SHARE + i, piece_of, chunk)
    chunk = chunk.astype(BF16)
    for half in (0, 1):
        buf2[half, here[half] * N + here[1 - half]] = chunk[:, half * HALF:(half + 1) * HALF]
    waits = gather_first(here, buf2, e_send, e_recv)
    left = solve(raw[...])
    left_ref[...] = left
    low_ref[...] = left.astype(BF16)
    for wait in waits:
        wait.wait_recv()
    gather_second(here, buf2, e_send, f_recv, lambda s: None)

    sums_of = []
    for half in (0, 1):
        total = jnp.zeros((16, HALF), F32)
        for i in range(N * N):
            total += buf2[half, i, PAD - 16:, :].astype(F32)
        sums_of.append(total[12:13] + total[13:14] + total[14:15])
    sq_t[t] = jnp.concatenate(sums_of + [jnp.zeros((6, HALF), F32)], axis=0)
    sent.append(begin(2, lambda p: sq_t.at[t], lambda i: sq_t.at[i], sq_t.at[seven], 6))

    group = 4 * SHARE
    n = lax.broadcasted_iota(jnp.int32, (group, 256), 0)
    k = lax.broadcasted_iota(jnp.int32, (group, 256), 1)
    skip = sum(jnp.where(n >= SHARE * i, PAD - SHARE, 0) for i in (1, 2, 3))
    close = jnp.where(k == n + skip, 1.0, 0.0).astype(BF16)
    for g in range(16):
        ys = range(g % 2 * 4, g % 2 * 4 + 4)
        wider = jnp.concatenate([chunks(buf2, half, g // 2, ys) for half in (0, 1)], axis=1)
        packed_ref[g * group:(g + 1) * group, :] = jnp.dot(
            close, wider, preferred_element_type=F32
        ).astype(BF16)

    sent[-1].wait_recv()
    total = added(sq_t)
    scale = lax.rsqrt(total / FF + 1e-06)
    right = jnp.concatenate(
        [right[:, :HALF] * scale[0:1, :], right[:, HALF:] * scale[1:2, :]], axis=1
    )
    right_ref[...] = right[:SHARE, :].astype(BF16)
    for wait in sent + share_waits:
        wait.wait_send()
    gather_sent(here, buf, a_send, a_recv)
    gather_sent(here, buf2, e_send, e_recv)
    remote(land, land, r_send, r_recv.at[0, 0], *ring_peer(here, 0, 0)).wait_send()


def sums(momentum, right_prev):
    dma = pltpu.SemaphoreType.DMA
    return pl.pallas_call(
        sums_kernel,
        out_shape=(
            jax.ShapeDtypeStruct((ROWS, RANK), F32),
            jax.ShapeDtypeStruct((ROWS, RANK), BF16),
            jax.ShapeDtypeStruct((COLS, RANK), BF16),
            jax.ShapeDtypeStruct((SHARE, RANK), BF16),
        ),
        in_specs=[pl.BlockSpec(memory_space=pltpu.HBM)] * 2,
        out_specs=[pl.BlockSpec(memory_space=pltpu.VMEM)] * 4,
        scratch_shapes=[
            pltpu.VMEM((ROWS, COLS), BF16),
            pltpu.VMEM((SHARE, RANK), BF16),
            pltpu.VMEM((2, N * N, PAD, HALF), BF16),
            pltpu.VMEM((2, N * N, PAD, HALF), BF16),
            pltpu.VMEM((ROWS, 64 * PAD), BF16),
            pltpu.VMEM((64 * PAD, ROWS), BF16),
            pltpu.VMEM((ROWS, RANK), F32),
            pltpu.VMEM((ROWS, RANK), F32),
            pltpu.VMEM((N, ROWS // N, RANK), F32),
            pltpu.VMEM((64, 8, 128), F32),
            pltpu.VMEM((64, 8, 128), F32),
            pltpu.VMEM((N, 8, 128), F32),
            pltpu.VMEM((N, 8, 128), F32),
            pltpu.VMEM((RANK, RANK), F32),
            pltpu.VMEM((2, N, N, PAD, HALF), F32),
            pltpu.VMEM((2, 14, 4, PAD, HALF), F32),
            pltpu.VMEM((2, N, PAD, HALF), F32),
            pltpu.VMEM((2, N, PAD, HALF), F32),
            pltpu.VMEM((N, 8, 128), F32),
            dma((2,)),
            dma((2,)), dma((2,)), dma((2, 2, 4, 2)),
            dma((7,)), dma((7,)),
            dma((2,)), dma((2,)),
            dma((2,)), dma((2,)), dma((2, 2, 4, 2)),
            dma, dma((2, 14)),
        ],
        compiler_params=pltpu.CompilerParams(
            collective_id=0, has_side_effects=True, vmem_limit_bytes=VMEM_LIMIT
        ),
    )(momentum, right_prev)


STEP = 768


def correct_kernel(
    m_ref, left_ref, low_ref, packed_ref, share_ref, new_ref, factor_ref, right_ref, tile, sem
):
    copies = []
    for i in range(COLS // STEP):
        part = pl.ds(i * STEP, STEP)
        update = lax.dot_general(
            low_ref[...], packed_ref[part, :], (((1,), (1,)), ((), ())),
            preferred_element_type=F32,
        )
        tile[i] = (m_ref[:, part].astype(F32) - 0.5 * update).astype(BF16)
        copy = pltpu.make_async_copy(tile.at[i], new_ref.at[:, part], sem.at[i])
        copy.start()
        copies.append(copy)
    factor_ref[...] = math.sqrt(D) * left_ref[...]
    right_ref[...] = share_ref[...]
    for copy in copies:
        copy.wait()


def correct(momentum, left, low, packed, share):
    vmem = pl.BlockSpec(memory_space=pltpu.VMEM)
    return pl.pallas_call(
        correct_kernel,
        out_shape=(
            jax.ShapeDtypeStruct((ROWS, COLS), BF16),
            jax.ShapeDtypeStruct((ROWS, RANK), F32),
            jax.ShapeDtypeStruct((SHARE, RANK), BF16),
        ),
        in_specs=[vmem] * 5,
        out_specs=(pl.BlockSpec(memory_space=pl.ANY), vmem, vmem),
        scratch_shapes=[
            pltpu.VMEM((COLS // STEP, ROWS, STEP), BF16),
            pltpu.SemaphoreType.DMA((COLS // STEP,)),
        ],
        compiler_params=pltpu.CompilerParams(vmem_limit_bytes=12 * 1024 * 1024),
    )(momentum, left, low, packed, share)


def body(momentum, right_prev):
    left, low, packed, share = sums(momentum, right_prev)
    return correct(momentum, left, low, packed, share)


def solution(mesh):
    in_specs = (P("fsdp", "tensor"), P(("tensor", "fsdp"), None))
    out_specs = (P("fsdp", "tensor"), P("fsdp", None), P(("tensor", "fsdp"), None))
    return jax.shard_map(body, mesh=mesh, in_specs=in_specs, out_specs=out_specs, check_vma=False)
```

```python
import math

import jax
import jax.numpy as jnp
from jax import lax
from jax.experimental import pallas as pl
from jax.experimental.pallas import tpu as pltpu
from jax.sharding import PartitionSpec as P

D = 16384
FF = 30720
RANK = 256
ROWS = 256
COLS = 3840
SHARE = 60
PAD = 64
N = 8
HALF = 128
MESH = pl.DeviceIdType.MESH
F32 = jnp.float32
BF16 = jnp.bfloat16
HIGHEST = lax.Precision.HIGHEST
VMEM_LIMIT = 40 * 1024 * 1024


def place():
    f, t = lax.axis_index("fsdp"), lax.axis_index("tensor")
    return lax.div(f, N), lax.rem(f, N), t


def up(i, d):
    return lax.rem(i + d, N)


def remote(src, dst, send, recv, z, y, t):
    return pltpu.make_async_remote_copy(
        src_ref=src,
        dst_ref=dst,
        send_sem=send,
        recv_sem=recv,
        device_id=(z * N + y, t),
        device_id_type=MESH,
    )


def greet(z, y, t):
    barrier = pltpu.get_barrier_semaphore()
    for d in range(1, N):
        for there in ((z, up(y, d), t), (up(z, d), y, t), (z, y, up(t, d))):
            pl.semaphore_signal(
                barrier, inc=1, device_id=(there[0] * N + there[1], there[2]), device_id_type=MESH
            )


def greeted():
    pl.semaphore_wait(pltpu.get_barrier_semaphore(), 3 * (N - 1))


def exchange(axis, here, src_of, dst_of, view, send, recv):
    me = here[axis]
    for d in (4, 3, 5, 2, 6, 1, 7):
        there = list(here)
        there[axis] = up(me, d)
        remote(src_of(there[axis]), dst_of(me), send, recv, *there).start()
    return remote(view, view, send, recv, *there)


def strip(buf, half, i, unit):
    if half == 0:
        return buf.at[0, i, pl.ds(4 * unit, 4)]
    return buf.at[1, pl.ds(4 * unit, 4), i]


STREAMS = [(unit, half, way) for unit in (0, 1) for half in (0, 1) for way in (0, 1)]


def ring_peer(here, half, way):
    z, y, t = here
    step = 1 if way == 0 else N - 1
    return (up(z, step), y, t) if half == 0 else (z, up(y, step), t)


def gather_first(here, buf, one_send, one_recv):
    waits = []
    for half in (0, 1):
        base = here[half] * N
        own = buf.at[half, base + here[1 - half]]
        waits.append(exchange(
            1 - half, here, lambda p: own, lambda i: buf.at[half, base + i],
            buf.at[half, pl.ds(0, N - 1)], one_send.at[half], one_recv.at[half],
        ))
    return waits


def gather_second(here, buf, one_send, two_recv, after):
    def ring(half, way, s, unit, i):
        part = buf.at[half, pl.ds(pl.multiple_of(i * N + 4 * unit, 4), 4)]
        return remote(
            part, part, one_send.at[half], two_recv.at[half, way, s, unit],
            *ring_peer(here, half, way),
        )

    def arrived(half, way, s, unit):
        me = here[half]
        i = up(me, N - 1 - s) if way == 0 else up(me, 1 + s)
        ring(half, way, s, unit, i).wait_recv()

    for s in range(4):
        for unit, half, way in STREAMS:
            if s == 3 and unit != way:
                continue
            if s > 0:
                arrived(half, way, s - 1, unit)
            me = here[half]
            ring(half, way, s, unit, up(me, N - s) if way == 0 else up(me, s)).start()
        after(s)
    for s in (2, 3):
        for unit, half, way in STREAMS:
            if (unit == way) == (s == 3):
                arrived(half, way, s, unit)


def gather_sent(here, buf, one_send, one_recv):
    for half in (0, 1):
        view = buf.at[half, pl.ds(0, N * N - 1)]
        remote(view, view, one_send.at[half], one_recv.at[half], *ring_peer(here, half, 0)).wait_send()


def chunks(buf, half, z, ys):
    if half == 0:
        return buf[0, z * N + ys[0]:z * N + ys[-1] + 1].reshape(len(ys) * PAD, HALF)
    return jnp.concatenate([buf[1, y * N + z] for y in ys], axis=0)


def spread(offset, transposed):
    shape = (HALF, 256) if transposed else (256, HALF)
    n = lax.broadcasted_iota(jnp.int32, shape, 0 if transposed else 1)
    k = lax.broadcasted_iota(jnp.int32, shape, 1 if transposed else 0)
    high = n >= PAD
    want = offset + n - jnp.where(high, PAD - SHARE, 0)
    inside = n - jnp.where(high, PAD, 0) < SHARE
    return jnp.where((k == want) & inside, 1.0, 0.0).astype(BF16)


def invert_cholesky(w, between):
    lane = lax.broadcasted_iota(jnp.int32, (8, 128), 1)
    sub = lax.broadcasted_iota(jnp.int32, (8, 128), 0)
    row_of = lambda v, k: jnp.broadcast_to(v[k:k + 1, :], (8, 128))
    depth = 32
    for p in range(RANK // depth):
        base = p * depth
        b0 = base // 128
        rows = [
            [w[base + 8 * a:base + 8 * a + 8, 128 * b:128 * b + 128] for b in (0, 1)]
            for a in range(depth // 8)
        ]
        for q in range(depth // 8):
            l0 = (base + 8 * q) % 128
            below = range(q, depth // 8)
            cols = {
                a: [
                    jnp.broadcast_to(rows[a][b0][:, l0 + k:l0 + k + 1], (8, 128))
                    for k in range(8)
                ]
                for a in below
            }
            for k in range(8):
                inv = lax.rsqrt(row_of(cols[q][k], k))
                here = lane == l0 + k
                fresh = [row_of(rows[q][b], k) for b in (0, 1)]
                fresh[b0] = jnp.where(here, 1.0, fresh[b0])
                fresh = [v * inv for v in fresh]
                scaled = {k2: row_of(cols[q][k2], k) * inv for k2 in range(k + 1, 8)}
                for a in below:
                    mult = cols[a][k] * inv
                    if a == q:
                        mult = jnp.where(sub > k, mult, 0.0)
                    for b in (0, 1):
                        old = rows[a][b]
                        if b == b0:
                            erase = here & (sub > k) if a == q else here
                            old = jnp.where(erase, 0.0, old)
                        new = old - mult * fresh[b]
                        if a == q:
                            new = jnp.where(sub == k, fresh[b], new)
                        rows[a][b] = new
                    for k2 in range(k + 1, 8):
                        cols[a][k2] = cols[a][k2] - mult * scaled[k2]
        panel = jnp.concatenate([jnp.concatenate(r, axis=1) for r in rows], axis=0)
        w[base:base + depth, :] = panel
        end = base + depth
        if end < RANK:
            first_row = end // 128 * 128
            at = lax.broadcasted_iota(jnp.int32, (depth, RANK), 1) - base
            over = (at > lax.broadcasted_iota(jnp.int32, (depth, RANK), 0)) & (at < depth)
            update = lax.dot_general(
                panel[:, first_row:], jnp.where(over, 0.0, panel), (((0,), (0,)), ((), ())),
                precision=HIGHEST, preferred_element_type=F32,
            )[end - first_row:, :]
            col = lax.broadcasted_iota(jnp.int32, (RANK - end, RANK), 1)
            old = jnp.where((col >= base) & (col < end), 0.0, w[end:, :])
            w[end:, :] = old - update
        between(p)


def sums_kernel(
    m_hbm, r_hbm, left_ref, low_ref, packed_ref, right_ref,
    m_ref, r_ref, buf, buf2, mpad, wide, part, raw, got, gram, summed, tile_y, tile_z, w, terms, land,
    near, rest, sq_t,
    load, a_send, a_recv, b_recv, c_send, c_recv, d_send, d_recv,
    e_send, e_recv, f_recv, r_send, r_recv,
):
    here = place()
    z, y, t = here
    load_r = pltpu.make_async_copy(r_hbm, r_ref, load.at[0])
    load_m = pltpu.make_async_copy(m_hbm, m_ref, load.at[1])
    load_r.start()
    load_m.start()
    greet(z, y, t)
    load_r.wait()
    n = lax.broadcasted_iota(jnp.int32, (PAD, SHARE), 0)
    k = lax.broadcasted_iota(jnp.int32, (PAD, SHARE), 1)
    longer = jnp.where(n == k, 1.0, 0.0).astype(BF16)
    own = jnp.dot(longer, r_ref[...], preferred_element_type=F32).astype(BF16)
    for half in (0, 1):
        buf[half, here[half] * N + here[1 - half]] = own[:, half * HALF:(half + 1) * HALF]
    greeted()
    waits = gather_first(here, buf, a_send, a_recv)

    load_m.wait()

    def widen(tiles, transposed):
        for i in tiles:
            start = min(120 * i // 128 * 128, COLS - 256)
            window = m_ref[:, start:start + 256]
            if transposed:
                wide[i * 128:(i + 1) * 128, :] = lax.dot_general(
                    spread(120 * i - start, True), window, (((1,), (1,)), ((), ())),
                    preferred_element_type=F32,
                ).astype(BF16)
            else:
                mpad[:, i * 128:(i + 1) * 128] = jnp.dot(
                    window, spread(120 * i - start, False), preferred_element_type=F32
                ).astype(BF16)

    widen(range(16), False)
    for wait in waits:
        wait.wait_recv()

    def beside(s):
        if s == 0:
            widen(range(16, 32), False)
        else:
            widen(range(11 * s - 11, min(11 * s, 32)), True)

    gather_second(here, buf, a_send, b_recv, beside)

    width = N * PAD
    total = jnp.zeros((ROWS, RANK), F32)
    for i in range(N):
        block = jnp.concatenate([chunks(buf, half, i, range(N)) for half in (0, 1)], axis=1)
        total += jnp.dot(
            mpad[:, i * width:(i + 1) * width], block, preferred_element_type=F32
        )
    part[...] = total

    def begin(axis, src_of, dst_of, view, k):
        return exchange(axis, here, src_of, dst_of, view, c_send.at[k], c_recv.at[k])

    def added(tiles):
        total = tiles[0]
        for i in range(1, N):
            total += tiles[i]
        return total

    rows = ROWS // N
    piece = lambda i: pl.ds(pl.multiple_of(i * rows, rows), rows)
    seven = pl.ds(0, N - 1)
    sent = [begin(2, lambda p: part.at[piece(p)], lambda i: got.at[i], got.at[seven], 0)]
    got[t] = part[piece(t), :]
    sent[-1].wait_recv()
    raw[piece(t), :] = added(got)
    sent.append(begin(
        2, lambda p: raw.at[piece(t)], lambda i: raw.at[piece(i)], raw.at[pl.ds(0, 7 * rows)], 1
    ))
    sent[-1].wait_recv()

    rows_all = raw[...]
    product = lax.dot_general(
        rows_all, rows_all, (((0,), (0,)), ((), ())),
        precision=HIGHEST, preferred_element_type=F32,
    )
    for i in range(64):
        r, c = i // 2 * 8, i % 2 * 128
        gram[i] = product[r:r + 8, c:c + 128]
    own_tile = t * N + y
    sent.append(begin(
        1, lambda p: gram.at[t * N + p], lambda i: tile_y.at[i], tile_y.at[seven], 2
    ))
    tile_y[y] = gram[own_tile]

    high = rows_all.astype(BF16)
    rows_all = rows_all - high.astype(F32)
    middle = rows_all.astype(BF16)
    lowest = (rows_all - middle.astype(F32)).astype(BF16)
    for i in range(N):
        block = wide[i * width:(i + 1) * width, :]
        total = jnp.dot(block, lowest, preferred_element_type=F32)
        total += jnp.dot(block, middle, preferred_element_type=F32)
        total += jnp.dot(block, high, preferred_element_type=F32)
        for half in (0, 1):
            terms[half, i] = total[:, half * HALF:(half + 1) * HALF].reshape(N, PAD, HALF)

    def order(way):
        a, b = way, 1 - way
        return ((0, a), (1, b), (1, a), (2, b), (2, a), (3, b), (3, a))

    def ring_copy(half, way, k, src):
        return remote(
            src, land.at[half, way * 7 + k], r_send, r_recv.at[half, way * 7 + k],
            *ring_peer(here, half, way),
        )

    def own_term(half, way, s, unit):
        me = here[half]
        return strip(terms, half, up(me, 4 - s) if way == 0 else up(me, 4 + s), unit)

    def tick(k):
        for half in (0, 1):
            for way in (0, 1):
                s, unit = order(way)[k]
                slot = land.at[half, way * 7 + k]
                ring_copy(half, way, k, slot).wait_recv()
                if s < 3:
                    slot[...] = slot[...] + own_term(half, way, s + 1, unit)[...]
                    ring_copy(half, way, k + 2, slot).start()
                elif k == 5:
                    mine = strip(terms, half, here[half], unit)
                    near[half, pl.ds(4 * unit, 4)] = mine[...] + slot[...]
                else:
                    near[half, pl.ds(4 * unit, 4)] = near[half, pl.ds(4 * unit, 4)] + slot[...]

    def ring_start(k):
        for half in (0, 1):
            for way in (0, 1):
                s, unit = order(way)[k]
                ring_copy(half, way, k, own_term(half, way, s, unit)).start()

    ring_start(0)
    ring_start(1)
    sent[-1].wait_recv()
    tile_z[z] = added(tile_y)
    sent.append(begin(
        0, lambda p: tile_z.at[z], lambda i: tile_z.at[i], tile_z.at[seven], 3
    ))
    tick(0)
    sent[-1].wait_recv()
    summed[own_tile] = added(tile_z)
    sent.append(begin(
        1, lambda p: summed.at[own_tile], lambda i: summed.at[t * N + i], summed.at[seven], 4
    ))
    tick(1)
    sent[-1].wait_recv()
    block = lambda i: summed.at[pl.ds(pl.multiple_of(i * N, N), N)]
    sent.append(begin(
        2, lambda p: block(t), lambda i: block(i), summed.at[pl.ds(0, 7 * N)], 5
    ))
    tick(2)
    tick(3)
    sent[-1].wait_recv()

    for i in range(64):
        r, c = i // 2 * 8, i % 2 * 128
        w[r:r + 8, c:c + 128] = summed[i]
    share_waits = []

    def between(p):
        if p < 3:
            tick(4 + p)
        if p == 2:
            for half in (0, 1):
                share_waits.append(exchange(
                    1 - half, here, lambda q: near.at[half, q], lambda i: rest.at[half, i],
                    rest.at[half, seven], d_send.at[half], d_recv.at[half],
                ))
                rest[half, here[1 - half]] = near[half, here[1 - half]]

    invert_cholesky(w, between)
    row = lax.broadcasted_iota(jnp.int32, (RANK, RANK), 0)
    col = lax.broadcasted_iota(jnp.int32, (RANK, RANK), 1)
    w[...] = jnp.where(col <= row, w[...], 0.0)
    solve = lambda rows: lax.dot_general(
        rows, w[...], (((1,), (1,)), ((), ())), precision=HIGHEST, preferred_element_type=F32
    )
    for wait in share_waits:
        wait.wait_recv()
    right = solve(jnp.concatenate([added(rest.at[0]), added(rest.at[1])], axis=1))

    squares = jnp.sum(right * right, axis=0, keepdims=True)
    row = lax.broadcasted_iota(jnp.int32, (PAD, RANK), 0)
    chunk = jnp.where(row < SHARE, right, 0.0)
    for i in range(3):
        piece_of = squares.astype(BF16).astype(F32)
        squares = squares - piece_of
        chunk = jnp.where(row == SHARE + i, piece_of, chunk)
    chunk = chunk.astype(BF16)
    for half in (0, 1):
        buf2[half, here[half] * N + here[1 - half]] = chunk[:, half * HALF:(half + 1) * HALF]
    waits = gather_first(here, buf2, e_send, e_recv)
    left = solve(raw[...])
    left_ref[...] = left
    low_ref[...] = left.astype(BF16)
    for wait in waits:
        wait.wait_recv()
    gather_second(here, buf2, e_send, f_recv, lambda s: None)

    sums_of = []
    for half in (0, 1):
        total = jnp.zeros((16, HALF), F32)
        for i in range(N * N):
            total += buf2[half, i, PAD - 16:, :].astype(F32)
        sums_of.append(total[12:13] + total[13:14] + total[14:15])
    sq_t[t] = jnp.concatenate(sums_of + [jnp.zeros((6, HALF), F32)], axis=0)
    sent.append(begin(2, lambda p: sq_t.at[t], lambda i: sq_t.at[i], sq_t.at[seven], 6))

    group = 4 * SHARE
    n = lax.broadcasted_iota(jnp.int32, (group, 256), 0)
    k = lax.broadcasted_iota(jnp.int32, (group, 256), 1)
    skip = sum(jnp.where(n >= SHARE * i, PAD - SHARE, 0) for i in (1, 2, 3))
    close = jnp.where(k == n + skip, 1.0, 0.0).astype(BF16)
    for g in range(16):
        ys = range(g % 2 * 4, g % 2 * 4 + 4)
        wider = jnp.concatenate([chunks(buf2, half, g // 2, ys) for half in (0, 1)], axis=1)
        packed_ref[g * group:(g + 1) * group, :] = jnp.dot(
            close, wider, preferred_element_type=F32
        ).astype(BF16)

    sent[-1].wait_recv()
    total = added(sq_t)
    scale = lax.rsqrt(total / FF + 1e-06)
    right = jnp.concatenate(
        [right[:, :HALF] * scale[0:1, :], right[:, HALF:] * scale[1:2, :]], axis=1
    )
    right_ref[...] = right[:SHARE, :].astype(BF16)
    for wait in sent + share_waits:
        wait.wait_send()
    gather_sent(here, buf, a_send, a_recv)
    gather_sent(here, buf2, e_send, e_recv)
    remote(land, land, r_send, r_recv.at[0, 0], *ring_peer(here, 0, 0)).wait_send()


def sums(momentum, right_prev):
    dma = pltpu.SemaphoreType.DMA
    return pl.pallas_call(
        sums_kernel,
        out_shape=(
            jax.ShapeDtypeStruct((ROWS, RANK), F32),
            jax.ShapeDtypeStruct((ROWS, RANK), BF16),
            jax.ShapeDtypeStruct((COLS, RANK), BF16),
            jax.ShapeDtypeStruct((SHARE, RANK), BF16),
        ),
        in_specs=[pl.BlockSpec(memory_space=pltpu.HBM)] * 2,
        out_specs=[pl.BlockSpec(memory_space=pltpu.VMEM)] * 4,
        scratch_shapes=[
            pltpu.VMEM((ROWS, COLS), BF16),
            pltpu.VMEM((SHARE, RANK), BF16),
            pltpu.VMEM((2, N * N, PAD, HALF), BF16),
            pltpu.VMEM((2, N * N, PAD, HALF), BF16),
            pltpu.VMEM((ROWS, 64 * PAD), BF16),
            pltpu.VMEM((64 * PAD, ROWS), BF16),
            pltpu.VMEM((ROWS, RANK), F32),
            pltpu.VMEM((ROWS, RANK), F32),
            pltpu.VMEM((N, ROWS // N, RANK), F32),
            pltpu.VMEM((64, 8, 128), F32),
            pltpu.VMEM((64, 8, 128), F32),
            pltpu.VMEM((N, 8, 128), F32),
            pltpu.VMEM((N, 8, 128), F32),
            pltpu.VMEM((RANK, RANK), F32),
            pltpu.VMEM((2, N, N, PAD, HALF), F32),
            pltpu.VMEM((2, 14, 4, PAD, HALF), F32),
            pltpu.VMEM((2, N, PAD, HALF), F32),
            pltpu.VMEM((2, N, PAD, HALF), F32),
            pltpu.VMEM((N, 8, 128), F32),
            dma((2,)),
            dma((2,)), dma((2,)), dma((2, 2, 4, 2)),
            dma((7,)), dma((7,)),
            dma((2,)), dma((2,)),
            dma((2,)), dma((2,)), dma((2, 2, 4, 2)),
            dma, dma((2, 14)),
        ],
        compiler_params=pltpu.CompilerParams(
            collective_id=0, has_side_effects=True, vmem_limit_bytes=VMEM_LIMIT
        ),
    )(momentum, right_prev)


STEP = 768


def correct_kernel(
    m_ref, left_ref, low_ref, packed_ref, share_ref, new_ref, factor_ref, right_ref, tile, sem
):
    copies = []
    for i in range(COLS // STEP):
        part = pl.ds(i * STEP, STEP)
        update = lax.dot_general(
            low_ref[...], packed_ref[part, :], (((1,), (1,)), ((), ())),
            preferred_element_type=F32,
        )
        tile[i] = (m_ref[:, part].astype(F32) - 0.5 * update).astype(BF16)
        copy = pltpu.make_async_copy(tile.at[i], new_ref.at[:, part], sem.at[i])
        copy.start()
        copies.append(copy)
    factor_ref[...] = math.sqrt(D) * left_ref[...]
    right_ref[...] = share_ref[...]
    for copy in copies:
        copy.wait()


def correct(momentum, left, low, packed, share):
    vmem = pl.BlockSpec(memory_space=pltpu.VMEM)
    return pl.pallas_call(
        correct_kernel,
        out_shape=(
            jax.ShapeDtypeStruct((ROWS, COLS), BF16),
            jax.ShapeDtypeStruct((ROWS, RANK), F32),
            jax.ShapeDtypeStruct((SHARE, RANK), BF16),
        ),
        in_specs=[vmem] * 5,
        out_specs=(pl.BlockSpec(memory_space=pl.ANY), vmem, vmem),
        scratch_shapes=[
            pltpu.VMEM((COLS // STEP, ROWS, STEP), BF16),
            pltpu.SemaphoreType.DMA((COLS // STEP,)),
        ],
        compiler_params=pltpu.CompilerParams(vmem_limit_bytes=12 * 1024 * 1024),
    )(momentum, left, low, packed, share)


def body(momentum, right_prev):
    left, low, packed, share = sums(momentum, right_prev)
    return correct(momentum, left, low, packed, share)


def solution(mesh):
    in_specs = (P("fsdp", "tensor"), P(("tensor", "fsdp"), None))
    out_specs = (P("fsdp", "tensor"), P("fsdp", None), P(("tensor", "fsdp"), None))
    return jax.shard_map(body, mesh=mesh, in_specs=in_specs, out_specs=out_specs, check_vma=False)
```

```python
import math

import jax
import jax.numpy as jnp
from jax import lax
from jax.experimental import pallas as pl
from jax.experimental.pallas import tpu as pltpu
from jax.sharding import PartitionSpec as P

D = 16384
FF = 30720
RANK = 256
ROWS = 256
COLS = 3840
SHARE = 60
PAD = 64
N = 8
HALF = 128
MESH = pl.DeviceIdType.MESH
F32 = jnp.float32
BF16 = jnp.bfloat16
HIGHEST = lax.Precision.HIGHEST
VMEM_LIMIT = 40 * 1024 * 1024


def place():
    f, t = lax.axis_index("fsdp"), lax.axis_index("tensor")
    return lax.div(f, N), lax.rem(f, N), t


def up(i, d):
    return lax.rem(i + d, N)


def remote(src, dst, send, recv, z, y, t):
    return pltpu.make_async_remote_copy(
        src_ref=src,
        dst_ref=dst,
        send_sem=send,
        recv_sem=recv,
        device_id=(z * N + y, t),
        device_id_type=MESH,
    )


def greet(z, y, t):
    barrier = pltpu.get_barrier_semaphore()
    for d in range(1, N):
        for there in ((z, up(y, d), t), (up(z, d), y, t), (z, y, up(t, d))):
            pl.semaphore_signal(
                barrier, inc=1, device_id=(there[0] * N + there[1], there[2]), device_id_type=MESH
            )


def greeted():
    pl.semaphore_wait(pltpu.get_barrier_semaphore(), 3 * (N - 1))


def exchange(axis, here, src_of, dst_of, view, send, recv):
    me = here[axis]
    for d in (4, 3, 5, 2, 6, 1, 7):
        there = list(here)
        there[axis] = up(me, d)
        remote(src_of(there[axis]), dst_of(me), send, recv, *there).start()
    return remote(view, view, send, recv, *there)


def strip(buf, half, i, unit):
    if half == 0:
        return buf.at[0, i, pl.ds(4 * unit, 4)]
    return buf.at[1, pl.ds(4 * unit, 4), i]


STREAMS = [(unit, half, way) for unit in (0, 1) for half in (0, 1) for way in (0, 1)]


def ring_peer(here, half, way):
    z, y, t = here
    step = 1 if way == 0 else N - 1
    return (up(z, step), y, t) if half == 0 else (z, up(y, step), t)


def gather_first(here, buf, one_send, one_recv):
    waits = []
    for half in (0, 1):
        base = here[half] * N
        own = buf.at[half, base + here[1 - half]]
        waits.append(exchange(
            1 - half, here, lambda p: own, lambda i: buf.at[half, base + i],
            buf.at[half, pl.ds(0, N - 1)], one_send.at[half], one_recv.at[half],
        ))
    return waits


def gather_second(here, buf, one_send, two_recv, after):
    def ring(half, way, s, unit, i):
        part = buf.at[half, pl.ds(pl.multiple_of(i * N + 4 * unit, 4), 4)]
        return remote(
            part, part, one_send.at[half], two_recv.at[half, way, s, unit],
            *ring_peer(here, half, way),
        )

    def arrived(half, way, s, unit):
        me = here[half]
        i = up(me, N - 1 - s) if way == 0 else up(me, 1 + s)
        ring(half, way, s, unit, i).wait_recv()

    for s in range(4):
        for unit, half, way in STREAMS:
            if s == 3 and unit != way:
                continue
            if s > 0:
                arrived(half, way, s - 1, unit)
            me = here[half]
            ring(half, way, s, unit, up(me, N - s) if way == 0 else up(me, s)).start()
        after(s)
    for s in (2, 3):
        for unit, half, way in STREAMS:
            if (unit == way) == (s == 3):
                arrived(half, way, s, unit)


def gather_sent(here, buf, one_send, one_recv):
    for half in (0, 1):
        view = buf.at[half, pl.ds(0, N * N - 1)]
        remote(view, view, one_send.at[half], one_recv.at[half], *ring_peer(here, half, 0)).wait_send()


def chunks(buf, half, z, ys):
    if half == 0:
        return buf[0, z * N + ys[0]:z * N + ys[-1] + 1].reshape(len(ys) * PAD, HALF)
    return jnp.concatenate([buf[1, y * N + z] for y in ys], axis=0)


def spread(offset, transposed):
    shape = (HALF, 256) if transposed else (256, HALF)
    n = lax.broadcasted_iota(jnp.int32, shape, 0 if transposed else 1)
    k = lax.broadcasted_iota(jnp.int32, shape, 1 if transposed else 0)
    high = n >= PAD
    want = offset + n - jnp.where(high, PAD - SHARE, 0)
    inside = n - jnp.where(high, PAD, 0) < SHARE
    return jnp.where((k == want) & inside, 1.0, 0.0).astype(BF16)


def invert_cholesky(w, between):
    lane = lax.broadcasted_iota(jnp.int32, (8, 128), 1)
    sub = lax.broadcasted_iota(jnp.int32, (8, 128), 0)
    row_of = lambda v, k: jnp.broadcast_to(v[k:k + 1, :], (8, 128))
    depth = 32
    for p in range(RANK // depth):
        base = p * depth
        b0 = base // 128
        rows = [
            [w[base + 8 * a:base + 8 * a + 8, 128 * b:128 * b + 128] for b in (0, 1)]
            for a in range(depth // 8)
        ]
        for q in range(depth // 8):
            l0 = (base + 8 * q) % 128
            below = range(q, depth // 8)
            cols = {
                a: [
                    jnp.broadcast_to(rows[a][b0][:, l0 + k:l0 + k + 1], (8, 128))
                    for k in range(8)
                ]
                for a in below
            }
            for k in range(8):
                inv = lax.rsqrt(row_of(cols[q][k], k))
                here = lane == l0 + k
                fresh = [row_of(rows[q][b], k) for b in (0, 1)]
                fresh[b0] = jnp.where(here, 1.0, fresh[b0])
                fresh = [v * inv for v in fresh]
                scaled = {k2: row_of(cols[q][k2], k) * inv for k2 in range(k + 1, 8)}
                for a in below:
                    mult = cols[a][k] * inv
                    if a == q:
                        mult = jnp.where(sub > k, mult, 0.0)
                    for b in (0, 1):
                        old = rows[a][b]
                        if b == b0:
                            erase = here & (sub > k) if a == q else here
                            old = jnp.where(erase, 0.0, old)
                        new = old - mult * fresh[b]
                        if a == q:
                            new = jnp.where(sub == k, fresh[b], new)
                        rows[a][b] = new
                    for k2 in range(k + 1, 8):
                        cols[a][k2] = cols[a][k2] - mult * scaled[k2]
        panel = jnp.concatenate([jnp.concatenate(r, axis=1) for r in rows], axis=0)
        w[base:base + depth, :] = panel
        end = base + depth
        if end < RANK:
            first_row = end // 128 * 128
            at = lax.broadcasted_iota(jnp.int32, (depth, RANK), 1) - base
            over = (at > lax.broadcasted_iota(jnp.int32, (depth, RANK), 0)) & (at < depth)
            update = lax.dot_general(
                panel[:, first_row:], jnp.where(over, 0.0, panel), (((0,), (0,)), ((), ())),
                precision=HIGHEST, preferred_element_type=F32,
            )[end - first_row:, :]
            col = lax.broadcasted_iota(jnp.int32, (RANK - end, RANK), 1)
            old = jnp.where((col >= base) & (col < end), 0.0, w[end:, :])
            w[end:, :] = old - update
        between(p)


def sums_kernel(
    m_hbm, r_ref, left_ref, low_ref, packed_ref, right_ref,
    m_ref, buf, buf2, mpad, wide, part, raw, got, gram, summed, tile_y, tile_z, w, terms, land,
    near, rest, sq_t,
    load, a_send, a_recv, b_recv, c_send, c_recv, d_send, d_recv,
    e_send, e_recv, f_recv, r_send, r_recv,
):
    here = place()
    z, y, t = here
    load_m = pltpu.make_async_copy(m_hbm, m_ref, load)
    load_m.start()
    greet(z, y, t)
    n = lax.broadcasted_iota(jnp.int32, (PAD, SHARE), 0)
    k = lax.broadcasted_iota(jnp.int32, (PAD, SHARE), 1)
    longer = jnp.where(n == k, 1.0, 0.0).astype(BF16)
    own = jnp.dot(longer, r_ref[...], preferred_element_type=F32).astype(BF16)
    for half in (0, 1):
        buf[half, here[half] * N + here[1 - half]] = own[:, half * HALF:(half + 1) * HALF]
    greeted()
    waits = gather_first(here, buf, a_send, a_recv)

    load_m.wait()

    def widen(tiles, transposed):
        for i in tiles:
            start = min(120 * i // 128 * 128, COLS - 256)
            window = m_ref[:, start:start + 256]
            if transposed:
                wide[i * 128:(i + 1) * 128, :] = lax.dot_general(
                    spread(120 * i - start, True), window, (((1,), (1,)), ((), ())),
                    preferred_element_type=F32,
                ).astype(BF16)
            else:
                mpad[:, i * 128:(i + 1) * 128] = jnp.dot(
                    window, spread(120 * i - start, False), preferred_element_type=F32
                ).astype(BF16)

    widen(range(16), False)
    for wait in waits:
        wait.wait_recv()

    def beside(s):
        if s == 0:
            widen(range(16, 32), False)
        else:
            widen(range(11 * s - 11, min(11 * s, 32)), True)

    gather_second(here, buf, a_send, b_recv, beside)

    width = N * PAD
    total = jnp.zeros((ROWS, RANK), F32)
    for i in range(N):
        block = jnp.concatenate([chunks(buf, half, i, range(N)) for half in (0, 1)], axis=1)
        total += jnp.dot(
            mpad[:, i * width:(i + 1) * width], block, preferred_element_type=F32
        )
    part[...] = total

    def begin(axis, src_of, dst_of, view, k):
        return exchange(axis, here, src_of, dst_of, view, c_send.at[k], c_recv.at[k])

    def added(tiles):
        total = tiles[0]
        for i in range(1, N):
            total += tiles[i]
        return total

    rows = ROWS // N
    piece = lambda i: pl.ds(pl.multiple_of(i * rows, rows), rows)
    seven = pl.ds(0, N - 1)
    sent = [begin(2, lambda p: part.at[piece(p)], lambda i: got.at[i], got.at[seven], 0)]
    got[t] = part[piece(t), :]
    sent[-1].wait_recv()
    raw[piece(t), :] = added(got)
    sent.append(begin(
        2, lambda p: raw.at[piece(t)], lambda i: raw.at[piece(i)], raw.at[pl.ds(0, 7 * rows)], 1
    ))
    sent[-1].wait_recv()

    rows_all = raw[...]
    product = lax.dot_general(
        rows_all, rows_all, (((0,), (0,)), ((), ())),
        precision=HIGHEST, preferred_element_type=F32,
    )
    for i in range(64):
        r, c = i // 2 * 8, i % 2 * 128
        gram[i] = product[r:r + 8, c:c + 128]
    own_tile = t * N + y
    sent.append(begin(
        1, lambda p: gram.at[t * N + p], lambda i: tile_y.at[i], tile_y.at[seven], 2
    ))
    tile_y[y] = gram[own_tile]

    high = rows_all.astype(BF16)
    rows_all = rows_all - high.astype(F32)
    middle = rows_all.astype(BF16)
    lowest = (rows_all - middle.astype(F32)).astype(BF16)
    for i in range(N):
        block = wide[i * width:(i + 1) * width, :]
        total = jnp.dot(block, lowest, preferred_element_type=F32)
        total += jnp.dot(block, middle, preferred_element_type=F32)
        total += jnp.dot(block, high, preferred_element_type=F32)
        for half in (0, 1):
            terms[half, i] = total[:, half * HALF:(half + 1) * HALF].reshape(N, PAD, HALF)

    def order(way):
        a, b = way, 1 - way
        return ((0, a), (1, b), (1, a), (2, b), (2, a), (3, b), (3, a))

    def ring_copy(half, way, k, src):
        return remote(
            src, land.at[half, way * 7 + k], r_send, r_recv.at[half, way * 7 + k],
            *ring_peer(here, half, way),
        )

    def own_term(half, way, s, unit):
        me = here[half]
        return strip(terms, half, up(me, 4 - s) if way == 0 else up(me, 4 + s), unit)

    def tick(k):
        for half in (0, 1):
            for way in (0, 1):
                s, unit = order(way)[k]
                slot = land.at[half, way * 7 + k]
                ring_copy(half, way, k, slot).wait_recv()
                if s < 3:
                    slot[...] = slot[...] + own_term(half, way, s + 1, unit)[...]
                    ring_copy(half, way, k + 2, slot).start()
                elif k == 5:
                    mine = strip(terms, half, here[half], unit)
                    near[half, pl.ds(4 * unit, 4)] = mine[...] + slot[...]
                else:
                    near[half, pl.ds(4 * unit, 4)] = near[half, pl.ds(4 * unit, 4)] + slot[...]

    def ring_start(k):
        for half in (0, 1):
            for way in (0, 1):
                s, unit = order(way)[k]
                ring_copy(half, way, k, own_term(half, way, s, unit)).start()

    ring_start(0)
    ring_start(1)
    sent[-1].wait_recv()
    tile_z[z] = added(tile_y)
    sent.append(begin(
        0, lambda p: tile_z.at[z], lambda i: tile_z.at[i], tile_z.at[seven], 3
    ))
    tick(0)
    sent[-1].wait_recv()
    summed[own_tile] = added(tile_z)
    sent.append(begin(
        1, lambda p: summed.at[own_tile], lambda i: summed.at[t * N + i], summed.at[seven], 4
    ))
    tick(1)
    sent[-1].wait_recv()
    block = lambda i: summed.at[pl.ds(pl.multiple_of(i * N, N), N)]
    sent.append(begin(
        2, lambda p: block(t), lambda i: block(i), summed.at[pl.ds(0, 7 * N)], 5
    ))
    tick(2)
    tick(3)
    sent[-1].wait_recv()

    for i in range(64):
        r, c = i // 2 * 8, i % 2 * 128
        w[r:r + 8, c:c + 128] = summed[i]
    share_waits = []

    def between(p):
        if p < 3:
            tick(4 + p)
        if p == 2:
            for half in (0, 1):
                share_waits.append(exchange(
                    1 - half, here, lambda q: near.at[half, q], lambda i: rest.at[half, i],
                    rest.at[half, seven], d_send.at[half], d_recv.at[half],
                ))
                rest[half, here[1 - half]] = near[half, here[1 - half]]

    invert_cholesky(w, between)
    row = lax.broadcasted_iota(jnp.int32, (RANK, RANK), 0)
    col = lax.broadcasted_iota(jnp.int32, (RANK, RANK), 1)
    w[...] = jnp.where(col <= row, w[...], 0.0)
    solve = lambda rows: lax.dot_general(
        rows, w[...], (((1,), (1,)), ((), ())), precision=HIGHEST, preferred_element_type=F32
    )
    for wait in share_waits:
        wait.wait_recv()
    right = solve(jnp.concatenate([added(rest.at[0]), added(rest.at[1])], axis=1))

    squares = jnp.sum(right * right, axis=0, keepdims=True)
    row = lax.broadcasted_iota(jnp.int32, (PAD, RANK), 0)
    chunk = jnp.where(row < SHARE, right, 0.0)
    for i in range(3):
        piece_of = squares.astype(BF16).astype(F32)
        squares = squares - piece_of
        chunk = jnp.where(row == SHARE + i, piece_of, chunk)
    chunk = chunk.astype(BF16)
    for half in (0, 1):
        buf2[half, here[half] * N + here[1 - half]] = chunk[:, half * HALF:(half + 1) * HALF]
    waits = gather_first(here, buf2, e_send, e_recv)
    left = solve(raw[...])
    left_ref[...] = left
    low_ref[...] = left.astype(BF16)
    for wait in waits:
        wait.wait_recv()
    gather_second(here, buf2, e_send, f_recv, lambda s: None)

    sums_of = []
    for half in (0, 1):
        total = jnp.zeros((16, HALF), F32)
        for i in range(N * N):
            total += buf2[half, i, PAD - 16:, :].astype(F32)
        sums_of.append(total[12:13] + total[13:14] + total[14:15])
    sq_t[t] = jnp.concatenate(sums_of + [jnp.zeros((6, HALF), F32)], axis=0)
    sent.append(begin(2, lambda p: sq_t.at[t], lambda i: sq_t.at[i], sq_t.at[seven], 6))

    group = 4 * SHARE
    n = lax.broadcasted_iota(jnp.int32, (group, 256), 0)
    k = lax.broadcasted_iota(jnp.int32, (group, 256), 1)
    skip = sum(jnp.where(n >= SHARE * i, PAD - SHARE, 0) for i in (1, 2, 3))
    close = jnp.where(k == n + skip, 1.0, 0.0).astype(BF16)
    for g in range(16):
        ys = range(g % 2 * 4, g % 2 * 4 + 4)
        wider = jnp.concatenate([chunks(buf2, half, g // 2, ys) for half in (0, 1)], axis=1)
        packed_ref[g * group:(g + 1) * group, :] = jnp.dot(
            close, wider, preferred_element_type=F32
        ).astype(BF16)

    sent[-1].wait_recv()
    total = added(sq_t)
    scale = lax.rsqrt(total / FF + 1e-06)
    right = jnp.concatenate(
        [right[:, :HALF] * scale[0:1, :], right[:, HALF:] * scale[1:2, :]], axis=1
    )
    right_ref[...] = right[:SHARE, :].astype(BF16)
    for wait in sent + share_waits:
        wait.wait_send()
    gather_sent(here, buf, a_send, a_recv)
    gather_sent(here, buf2, e_send, e_recv)
    remote(land, land, r_send, r_recv.at[0, 0], *ring_peer(here, 0, 0)).wait_send()


def sums(momentum, right_prev):
    dma = pltpu.SemaphoreType.DMA
    return pl.pallas_call(
        sums_kernel,
        out_shape=(
            jax.ShapeDtypeStruct((ROWS, RANK), F32),
            jax.ShapeDtypeStruct((ROWS, RANK), BF16),
            jax.ShapeDtypeStruct((COLS, RANK), BF16),
            jax.ShapeDtypeStruct((SHARE, RANK), BF16),
        ),
        in_specs=[pl.BlockSpec(memory_space=pltpu.HBM), pl.BlockSpec(memory_space=pltpu.VMEM)],
        out_specs=[pl.BlockSpec(memory_space=pltpu.VMEM)] * 4,
        scratch_shapes=[
            pltpu.VMEM((ROWS, COLS), BF16),
            pltpu.VMEM((2, N * N, PAD, HALF), BF16),
            pltpu.VMEM((2, N * N, PAD, HALF), BF16),
            pltpu.VMEM((ROWS, 64 * PAD), BF16),
            pltpu.VMEM((64 * PAD, ROWS), BF16),
            pltpu.VMEM((ROWS, RANK), F32),
            pltpu.VMEM((ROWS, RANK), F32),
            pltpu.VMEM((N, ROWS // N, RANK), F32),
            pltpu.VMEM((64, 8, 128), F32),
            pltpu.VMEM((64, 8, 128), F32),
            pltpu.VMEM((N, 8, 128), F32),
            pltpu.VMEM((N, 8, 128), F32),
            pltpu.VMEM((RANK, RANK), F32),
            pltpu.VMEM((2, N, N, PAD, HALF), F32),
            pltpu.VMEM((2, 14, 4, PAD, HALF), F32),
            pltpu.VMEM((2, N, PAD, HALF), F32),
            pltpu.VMEM((2, N, PAD, HALF), F32),
            pltpu.VMEM((N, 8, 128), F32),
            dma,
            dma((2,)), dma((2,)), dma((2, 2, 4, 2)),
            dma((7,)), dma((7,)),
            dma((2,)), dma((2,)),
            dma((2,)), dma((2,)), dma((2, 2, 4, 2)),
            dma, dma((2, 14)),
        ],
        compiler_params=pltpu.CompilerParams(
            collective_id=0, has_side_effects=True, vmem_limit_bytes=VMEM_LIMIT
        ),
    )(momentum, right_prev)


STEP = 768


def correct_kernel(
    m_ref, left_ref, low_ref, packed_ref, share_ref, new_ref, factor_ref, right_ref, tile, sem
):
    copies = []
    for i in range(COLS // STEP):
        part = pl.ds(i * STEP, STEP)
        update = lax.dot_general(
            low_ref[...], packed_ref[part, :], (((1,), (1,)), ((), ())),
            preferred_element_type=F32,
        )
        tile[i] = (m_ref[:, part].astype(F32) - 0.5 * update).astype(BF16)
        copy = pltpu.make_async_copy(tile.at[i], new_ref.at[:, part], sem.at[i])
        copy.start()
        copies.append(copy)
    factor_ref[...] = math.sqrt(D) * left_ref[...]
    right_ref[...] = share_ref[...]
    for copy in copies:
        copy.wait()


def correct(momentum, left, low, packed, share):
    vmem = pl.BlockSpec(memory_space=pltpu.VMEM)
    return pl.pallas_call(
        correct_kernel,
        out_shape=(
            jax.ShapeDtypeStruct((ROWS, COLS), BF16),
            jax.ShapeDtypeStruct((ROWS, RANK), F32),
            jax.ShapeDtypeStruct((SHARE, RANK), BF16),
        ),
        in_specs=[vmem] * 5,
        out_specs=(pl.BlockSpec(memory_space=pl.ANY), vmem, vmem),
        scratch_shapes=[
            pltpu.VMEM((COLS // STEP, ROWS, STEP), BF16),
            pltpu.SemaphoreType.DMA((COLS // STEP,)),
        ],
        compiler_params=pltpu.CompilerParams(vmem_limit_bytes=12 * 1024 * 1024),
    )(momentum, left, low, packed, share)


def body(momentum, right_prev):
    left, low, packed, share = sums(momentum, right_prev)
    return correct(momentum, left, low, packed, share)


def solution(mesh):
    in_specs = (P("fsdp", "tensor"), P(("tensor", "fsdp"), None))
    out_specs = (P("fsdp", "tensor"), P("fsdp", None), P(("tensor", "fsdp"), None))
    return jax.shard_map(body, mesh=mesh, in_specs=in_specs, out_specs=out_specs, check_vma=False)
```
